128 devices in a mesh: row: 32 (over y, z, core), col: 4 (over x).
Axes of the slice: x: 4, y: 4, z: 4, core: 2. Of those that a mesh axis runs over, the one named last changes fastest.
Arguments:
- tile_values: bfloat16 [5632, 4, 256, 256], P('row', 'col'), may hold values from -0.375 to 0.375
- tile_rows: int32 [5632, 4], P('row', 'col'), may hold values from 0 to 15, as said below
- tile_source: int32 [5632, 4], P('row', 'col'), may hold values from 0 to 31
- tile_slot: int32 [5632, 4], P('row', 'col'), may hold values from 0 to 1
- send_lists: int32 [32, 4, 32, 2], P('row', 'col'), may hold values from 0 to 7
- basis_blocks: bfloat16 [256, 4, 256, 256], P('row', 'col'), may hold values from -6 to 6
Outputs:
- new_basis: float32 [131072, 256], P(('row', 'col'))
- triangle: float32 [256, 256], replicated
The draws below stay inside these ranges and needn't reach their ends.
Inputs may be any that keep to these rules, and one draw needn't show every extreme that they name: `tile_rows`: in every slab and group each of the 16 block rows holds at least one tile.
All inputs are finite; a program needn't handle non-finite values.
Results may differ from the reference program's by a relative error of at most 0.0015.
Values may be sent and summed in bfloat16 or wider, within the bound.
No kernel may reach another device: no remote copies, remote signals or barrier semaphores. Data moves between devices by JAX's collectives and lax.ppermute only.
A program may use at most 256 MiB of HBM per device.

```python
import jax
import jax.numpy as jnp
from jax import lax

TILE = 256
RANK = 256
BR_DEV = 16
TILES_DEV = 176
FB_DEV = 8
SLOTS = 2
CELLS = 131072
N_ROW = 32
N_COL = 4


def draw_tile_rows(key, part):
    total = N_ROW * TILES_DEV
    key_a = jax.random.fold_in(key, 11)
    key_b = jax.random.fold_in(key, 12)
    key_c = jax.random.fold_in(key, 13)
    key_d = jax.random.fold_in(key, 14)
    offset = jax.random.randint(key_d, (N_ROW, 1, N_COL), 0, BR_DEV)
    offset = jnp.broadcast_to(offset, (N_ROW, TILES_DEV, N_COL)).reshape(total, N_COL)
    first = jax.random.randint(key_a, (total, N_COL), 0, BR_DEV)
    second = jax.random.randint(key_b, (total, N_COL), 0, BR_DEV)
    third = jax.random.randint(key_c, (total, N_COL), 0, BR_DEV)
    skewed = jnp.minimum(jnp.minimum(first, second), third)
    position = (jnp.arange(total, dtype=jnp.int32) % TILES_DEV)[:, None]
    base = jnp.where(position < BR_DEV, position, skewed)
    return ((base + offset) % BR_DEV).astype(jnp.int32)


def with_ends(entries, rng, least, high):
    spot = [jax.random.randint(jax.random.fold_in(rng, axis), (), 0, length) for axis, length in enumerate(entries.shape)]
    main_axis = entries.shape.index(max(entries.shape))
    beside = spot[:main_axis] + [(spot[main_axis] + 1) % entries.shape[main_axis]] + spot[main_axis + 1:]
    return entries.at[tuple(spot)].set(least).at[tuple(beside)].set(high)


def block_scale(own_key, extent, cuts, smallest, top_value):
    level, own = 1.0, jax.random.fold_in(own_key, 6)
    for axis_at, parts in cuts:
        steps = jnp.exp(jax.random.uniform(jax.random.fold_in(own, axis_at), (parts,), jnp.float32, smallest / len(cuts), top_value / len(cuts)))
        level = level * jnp.repeat(steps, extent[axis_at] // parts).reshape([-1 if axis == axis_at else 1 for axis in range(len(extent))])
    return level


def noise(own_key, shape, scale, bound, cuts=(), kind=jnp.bfloat16):
    entries = jax.random.normal(own_key, shape, jnp.float32) * scale
    if len(cuts) > 0:
        entries = block_scale(own_key, shape, cuts, -0.22, 0.18) * entries
    return jnp.clip(entries, min=-bound, max=bound).astype(kind)


def setup_inputs(seed: int = 0) -> dict:
    arg_keys = jax.random.split(jax.random.key(seed), 7)
    tile_values = noise(arg_keys[0], (N_ROW * TILES_DEV, N_COL, TILE, TILE), TILE ** -0.5, 0.375, ((0, 32), (1, 4)))
    tile_rows = draw_tile_rows(jax.random.fold_in(arg_keys[6], 71), 0)
    tile_source = with_ends(jax.random.randint(arg_keys[2], (N_ROW * TILES_DEV, N_COL), 0, N_ROW), jax.random.fold_in(arg_keys[2], 1), 0, N_ROW - 1).astype(jnp.int32)
    tile_slot = with_ends(jax.random.randint(arg_keys[3], (N_ROW * TILES_DEV, N_COL), 0, SLOTS), jax.random.fold_in(arg_keys[3], 1), 0, SLOTS - 1).astype(jnp.int32)
    send_lists = with_ends(jax.random.randint(arg_keys[4], (N_ROW, N_COL, N_ROW, SLOTS), 0, FB_DEV), jax.random.fold_in(arg_keys[4], 1), 0, FB_DEV - 1).astype(jnp.int32)
    basis_blocks = noise(arg_keys[5], (N_ROW * FB_DEV, N_COL, TILE, RANK), 1.0, 6.0, ((0, 32), (1, 4)))
    return dict(tile_values=tile_values, tile_rows=tile_rows, tile_source=tile_source, tile_slot=tile_slot, send_lists=send_lists, basis_blocks=basis_blocks)


def upper_factor(gram):
    width = gram.shape[0]
    index = jnp.arange(width, dtype=jnp.int32)

    def row_fill(j, upper):
        unit = (index == j).astype(jnp.float32)
        known = jnp.dot(upper, unit, precision=lax.Precision.HIGHEST)
        target = lax.dynamic_index_in_dim(gram, j, 0, keepdims=False)
        residue = target - jnp.dot(known, upper, precision=lax.Precision.HIGHEST)
        pivot = jnp.sqrt(lax.dynamic_index_in_dim(residue, j, 0, keepdims=False))
        filled = jnp.where(index >= j, residue / pivot, jnp.float32(0.0))
        return upper + unit[:, None] * filled[None, :]
    return lax.fori_loop(0, width, row_fill, jnp.zeros((width, width), jnp.float32))

def upper_inverse(upper):
    width = upper.shape[0]
    index = jnp.arange(width, dtype=jnp.int32)

    def row_step(step, inverse):
        i = (width - 1 - step).astype(jnp.int32)
        row_now = lax.dynamic_index_in_dim(upper, i, 0, keepdims=False)
        pivot = lax.dynamic_index_in_dim(row_now, i, 0, keepdims=False)
        unit = (index == i).astype(jnp.float32)
        solved = (unit - jnp.dot(row_now, inverse, precision=lax.Precision.HIGHEST)) / pivot
        return jnp.where((index == i)[:, None], solved[None, :], inverse)
    return lax.fori_loop(0, width, row_step, jnp.zeros((width, width), jnp.float32))

def slab_rows(tile_values, tile_rows, tile_source, tile_slot, send_lists, basis_blocks, slab_index):
    total = jnp.zeros((BR_DEV, TILE, RANK), jnp.float32)
    start = (slab_index * TILES_DEV).astype(jnp.int32)
    for group in range(N_COL):
        values = lax.dynamic_slice_in_dim(tile_values[:, group], start, TILES_DEV, 0)
        blocks_row = lax.dynamic_slice_in_dim(tile_rows[:, group], start, TILES_DEV, 0)
        source = lax.dynamic_slice_in_dim(tile_source[:, group], start, TILES_DEV, 0)
        slotted = lax.dynamic_slice_in_dim(tile_slot[:, group], start, TILES_DEV, 0)
        listed = send_lists[source, group, slab_index, slotted]
        chosen = basis_blocks[source * FB_DEV + listed, group]
        product = jnp.einsum('tij,tjk->tik', values.astype(jnp.float32), chosen.astype(jnp.float32), precision=lax.Precision.HIGHEST)
        total = total + jax.ops.segment_sum(product, blocks_row, num_segments=BR_DEV)
    return total

def reference(tile_values, tile_rows, tile_source, tile_slot, send_lists, basis_blocks):

    def one_slab(slab_index):
        return slab_rows(tile_values, tile_rows, tile_source, tile_slot, send_lists, basis_blocks, slab_index)
    whole_y = lax.map(one_slab, jnp.arange(N_ROW, dtype=jnp.int32)).reshape(CELLS, RANK)
    gram = jnp.dot(whole_y.T, whole_y, precision=lax.Precision.HIGHEST)
    upper = upper_factor(gram)
    scale = jnp.sqrt(jnp.float32(CELLS))
    solved = jnp.dot(whole_y, upper_inverse(upper), precision=lax.Precision.HIGHEST)
    return (solved * scale, upper / scale)
```

```python
import functools

import jax
import jax.numpy as jnp
from jax import lax
from jax.experimental import pallas as pl
from jax.experimental.pallas import tpu as pltpu
from jax.sharding import PartitionSpec as P

BR_DEV = 16
HALF = 128
GROUP = 8
STEP = 32704.0
LEAST = 2.0**-80
HIGHEST = lax.Precision.HIGHEST
F32 = jnp.float32


def pack_kernel(half, lists, owned, out, sems):
    count = out.shape[0]

    def one(i):
        return pltpu.make_async_copy(
            owned.at[lists[i], :, pl.ds(half * HALF, HALF)], out.at[i], sems.at[i]
        )

    for i in range(count):
        one(i).start()
    for i in range(count):
        one(i).wait()


def pack(lists, owned, half):
    count = lists.shape[0]
    height = owned.shape[1]
    return pl.pallas_call(
        functools.partial(pack_kernel, half),
        out_shape=jax.ShapeDtypeStruct((count, height, HALF), owned.dtype),
        in_specs=[
            pl.BlockSpec(memory_space=pltpu.SMEM),
            pl.BlockSpec(memory_space=pltpu.VMEM),
        ],
        out_specs=pl.BlockSpec(memory_space=pl.ANY),
        scratch_shapes=[pltpu.SemaphoreType.DMA((count,))],
        cost_estimate=pl.CostEstimate(
            flops=0, bytes_accessed=2 * count * height * HALF * 2, transcendentals=0
        ),
        name=f"pack{half}",
    )(lists, owned)


def encode(part):
    largest = jnp.max(jnp.abs(part), axis=0, keepdims=True)
    power = jnp.ceil(jnp.log2(jnp.maximum(largest, LEAST)))
    steps = jnp.floor(part * (jnp.exp2(-power) * STEP) + 0.5)
    return steps.astype(jnp.int32).astype(jnp.int16), power


def tiles_kernel(places, blocks, values, arrived, out, total):
    step = pl.program_id(0)

    @pl.when(step == 0)
    def _():
        total[...] = jnp.zeros_like(total)

    for u in range(GROUP):
        t = step * GROUP + u
        total[blocks[t]] += jnp.dot(values[u], arrived[places[t]], preferred_element_type=F32)

    @pl.when(step == pl.num_programs(0) - 1)
    def _():
        shares = out.shape[0]
        each = BR_DEV // shares
        for d in range(shares):
            part = total[d * each : (d + 1) * each]
            rows = each * part.shape[1]
            steps, power = encode(part.reshape(rows, HALF))
            out[d, pl.ds(0, rows)] = steps
            out[d, pl.ds(rows, 16)] = (
                jnp.broadcast_to(power, (16, HALF)).astype(jnp.int32).astype(jnp.int16)
            )


def tiles(places, blocks, values, arrived, shares, half):
    count, height, depth = values.shape
    rows = BR_DEV * height // shares
    return pl.pallas_call(
        tiles_kernel,
        grid_spec=pltpu.PrefetchScalarGridSpec(
            num_scalar_prefetch=2,
            grid=(count // GROUP,),
            in_specs=[
                pl.BlockSpec((GROUP, height, depth), lambda i, *_: (i, 0, 0)),
                pl.BlockSpec(arrived.shape, lambda i, *_: (0, 0, 0)),
            ],
            out_specs=pl.BlockSpec((shares, rows + 16, HALF), lambda i, *_: (0, 0, 0)),
            scratch_shapes=[pltpu.VMEM((BR_DEV, height, HALF), F32)],
        ),
        out_shape=jax.ShapeDtypeStruct((shares, rows + 16, HALF), jnp.int16),
        compiler_params=pltpu.CompilerParams(vmem_limit_bytes=40 * 2**20),
        cost_estimate=pl.CostEstimate(
            flops=2 * count * height * depth * HALF,
            bytes_accessed=count * height * depth * 2 + arrived.size * 2,
            transcendentals=0,
        ),
        name=f"tiles{half}",
    )(places, blocks, values, arrived)


def dot_t(a, b):
    return lax.dot_general(
        a, b, (((0,), (0,)), ((), ())), precision=HIGHEST, preferred_element_type=F32
    )


def dot_n(a, b):
    return jnp.dot(a, b, precision=HIGHEST, preferred_element_type=F32)


def dot_bt(a, b):
    return lax.dot_general(
        a, b, (((1,), (1,)), ((), ())), precision=HIGHEST, preferred_element_type=F32
    )


def decode(ref):
    shares, rows = ref.shape[0], ref.shape[1] - 16
    y = None
    for g in range(shares):
        power = ref[g, pl.ds(rows, 16)].astype(jnp.int32).astype(F32)[0:1]
        part = ref[g, pl.ds(0, rows)].astype(jnp.int32).astype(F32) * (
            jnp.exp2(power) * (1.0 / STEP)
        )
        y = part if y is None else y + part
    return y


def gram_kernel(*refs):
    (*before, coded, y_out, gram_out) = refs
    y = decode(coded)
    y_out[...] = y
    at = 0
    for ref in before:
        gram_out[pl.ds(at, HALF)] = dot_t(ref[...], y)
        at += HALF
    gram_out[pl.ds(at, HALF)] = dot_t(y, y)


def gram(coded, before):
    rows = coded.shape[1] - 16
    height = HALF * (len(before) + 1)
    return pl.pallas_call(
        gram_kernel,
        out_shape=(
            jax.ShapeDtypeStruct((rows, HALF), F32),
            jax.ShapeDtypeStruct((height, HALF), F32),
        ),
        compiler_params=pltpu.CompilerParams(vmem_limit_bytes=40 * 2**20),
        cost_estimate=pl.CostEstimate(
            flops=12 * rows * height * HALF, bytes_accessed=rows * HALF * 12, transcendentals=0
        ),
        name=f"gram{len(before)}",
    )(*before, coded)


def factor64(a):
    n = a.shape[0]
    row_at = lax.broadcasted_iota(jnp.int32, (n, n), 0)
    col_at = lax.broadcasted_iota(jnp.int32, (n, n), 1)
    unit = (row_at == col_at).astype(F32)
    wide = jnp.concatenate([a, unit], axis=1)
    strips = [wide[8 * i : 8 * i + 8] for i in range(n // 8)]
    in_strip = lax.broadcasted_iota(jnp.int32, (8, 2 * n), 0)
    for j in range(n):
        b, r = divmod(j, 8)
        row = strips[b][r : r + 1]
        scaled = row / row[:, j : j + 1]
        for i in range(b, n // 8):
            if i == b and r == 7:
                continue
            column = jnp.broadcast_to(strips[i][:, j : j + 1], (8, 2 * n))
            if i == b:
                column = jnp.where(in_strip > r, column, 0.0)
            strips[i] = strips[i] - column * scaled
    wide = jnp.concatenate(strips, axis=0)
    square, inverse = wide[:, :n], wide[:, n:]
    pivots = jnp.sum(jnp.where(row_at == col_at, square, 0.0), axis=1, keepdims=True)
    scale = 1.0 / jnp.sqrt(pivots)
    return (
        jnp.where(col_at >= row_at, square, 0.0) * scale,
        jnp.where(col_at <= row_at, inverse, 0.0) * scale,
    )


def factor128(a):
    n = a.shape[0] // 2
    r00, t00 = factor64(a[:n, :n])
    r01 = dot_n(t00, a[:n, n:])
    r11, t11 = factor64(a[n:, n:] - dot_t(r01, r01))
    t10 = -dot_n(t11, dot_n(r01.T, t00))
    none = jnp.zeros((n, n), F32)
    r = jnp.concatenate(
        [jnp.concatenate([r00, r01], axis=1), jnp.concatenate([none, r11], axis=1)], axis=0
    )
    t = jnp.concatenate(
        [jnp.concatenate([t00, none], axis=1), jnp.concatenate([t10, t11], axis=1)], axis=0
    )
    return r, t


def first_kernel(scale, g_ref, y_ref, r_out, t_out, z_out):
    r, t = factor128(g_ref[...])
    r_out[...] = r
    t_out[...] = t
    z_out[...] = dot_bt(y_ref[...], t)


def first(g, y, scale):
    return pl.pallas_call(
        functools.partial(first_kernel, scale),
        out_shape=(
            jax.ShapeDtypeStruct((HALF, HALF), F32),
            jax.ShapeDtypeStruct((HALF, HALF), F32),
            jax.ShapeDtypeStruct(y.shape, F32),
        ),
        compiler_params=pltpu.CompilerParams(vmem_limit_bytes=40 * 2**20),
        cost_estimate=pl.CostEstimate(
            flops=20 * 2**20 * 1000, bytes_accessed=8 * y.size, transcendentals=0
        ),
        name="first",
    )(g, y)


def last_kernel(scale, g_ref, r_ref, t_ref, z_ref, y_ref, basis_out, triangle_out):
    r01 = dot_n(t_ref[...], g_ref[pl.ds(0, HALF)])
    r11, t11 = factor128(g_ref[pl.ds(HALF, HALF)] - dot_t(r01, r01))
    z = z_ref[...]
    basis_out[:, pl.ds(0, HALF)] = z * scale
    basis_out[:, pl.ds(HALF, HALF)] = dot_bt(y_ref[...] - dot_n(z, r01), t11) * scale
    share = 1.0 / scale
    triangle_out[pl.ds(0, HALF), pl.ds(0, HALF)] = r_ref[...] * share
    triangle_out[pl.ds(0, HALF), pl.ds(HALF, HALF)] = r01 * share
    triangle_out[pl.ds(HALF, HALF), pl.ds(0, HALF)] = jnp.zeros((HALF, HALF), F32)
    triangle_out[pl.ds(HALF, HALF), pl.ds(HALF, HALF)] = r11 * share


def last(g, r, t, z, y, scale):
    return pl.pallas_call(
        functools.partial(last_kernel, scale),
        out_shape=(
            jax.ShapeDtypeStruct((y.shape[0], 2 * HALF), F32),
            jax.ShapeDtypeStruct((2 * HALF, 2 * HALF), F32),
        ),
        compiler_params=pltpu.CompilerParams(vmem_limit_bytes=40 * 2**20),
        name="last",
    )(g, r, t, z, y)


def sum_all(part):
    axes = ("row", "col")
    n = lax.axis_size("row") * lax.axis_size("col")
    height = part.shape[0]
    pieces = lax.all_to_all(part.reshape(n, height // n, HALF), axes, 0, 0, tiled=True)
    share = jnp.sum(pieces, axis=0, keepdims=True)
    copies = jnp.broadcast_to(share, (n, height // n, HALF))
    return lax.all_to_all(copies, axes, 0, 0, tiled=True).reshape(height, HALF)


def local(tile_values, tile_rows, tile_source, tile_slot, send_lists, basis_blocks):
    values = tile_values[:, 0]
    blocks = tile_rows[:, 0]
    slots = send_lists.shape[3]
    places = tile_source[:, 0] * slots + tile_slot[:, 0]
    lists = send_lists.reshape(-1)
    owned = basis_blocks[:, 0]
    rows, cols = lax.axis_size("row"), lax.axis_size("col")
    cells = BR_DEV * values.shape[1] * rows
    scale = float(cells) ** 0.5

    def product(half):
        arrived = lax.all_to_all(pack(lists, owned, half), "row", 0, 0, tiled=True)
        coded = tiles(places, blocks, values, arrived, cols, half)
        return lax.all_to_all(coded, "col", 0, 0, tiled=True)

    y0, g0 = gram(product(0), ())
    r, t, z = first(sum_all(g0), y0, scale)
    y1, g1 = gram(product(1), (y0,))
    return last(sum_all(g1), r, t, z, y1, scale)


def solution(mesh):
    return jax.shard_map(
        local,
        mesh=mesh,
        in_specs=(
            P("row", "col", None, None),
            P("row", "col"),
            P("row", "col"),
            P("row", "col"),
            P("row", "col", None, None),
            P("row", "col", None, None),
        ),
        out_specs=(P(("row", "col"), None), P()),
        check_vma=False,
    )
```

```python
import functools

import jax
import jax.numpy as jnp
from jax import lax
from jax.experimental import pallas as pl
from jax.experimental.pallas import tpu as pltpu
from jax.sharding import PartitionSpec as P

BR_DEV = 16
HALF = 128
GROUP = 88
LOADS = 22
STEP = 32704.0
LEAST = 2.0**-80
HIGHEST = lax.Precision.HIGHEST
F32 = jnp.float32


def pack_kernel(half, lists, owned, out, sems):
    count = out.shape[0]

    def one(i):
        return pltpu.make_async_copy(
            owned.at[lists[i], :, pl.ds(half * HALF, HALF)], out.at[i], sems.at[i]
        )

    for i in range(count):
        one(i).start()
    for i in range(count):
        one(i).wait()


def pack(lists, owned, half):
    count = lists.shape[0]
    height = owned.shape[1]
    return pl.pallas_call(
        functools.partial(pack_kernel, half),
        out_shape=jax.ShapeDtypeStruct((count, height, HALF), owned.dtype),
        in_specs=[
            pl.BlockSpec(memory_space=pltpu.SMEM),
            pl.BlockSpec(memory_space=pltpu.VMEM),
        ],
        out_specs=pl.BlockSpec(memory_space=pl.ANY),
        scratch_shapes=[pltpu.SemaphoreType.DMA((count,))],
        cost_estimate=pl.CostEstimate(
            flops=0, bytes_accessed=2 * count * height * HALF * 2, transcendentals=0
        ),
        name=f"pack{half}",
    )(lists, owned)


def encode(part):
    largest = jnp.max(jnp.abs(part), axis=0, keepdims=True)
    power = jnp.ceil(jnp.log2(jnp.maximum(largest, LEAST)))
    steps = jnp.floor(part * (jnp.exp2(-power) * STEP) + 0.5)
    return steps.astype(jnp.int32).astype(jnp.int16), power


def tiles_kernel(shares, me, places, blocks, values_hbm, arrived_hbm, *refs):
    *_, total, values, arrived, value_sems, arrived_sems = refs
    outs = refs[-5 - shares : -5]
    count, loads, parts = values.shape[0], value_sems.shape[0], arrived_sems.shape[0]

    def bring(i):
        part = pl.ds(i * (count // loads), count // loads)
        return pltpu.make_async_copy(values_hbm.at[part], values.at[part], value_sems.at[i])

    def bring_basis(i):
        part = pl.ds(i * (arrived.shape[0] // parts), arrived.shape[0] // parts)
        return pltpu.make_async_copy(arrived_hbm.at[part], arrived.at[part], arrived_sems.at[i])

    for i in range(parts):
        bring_basis(i).start()
    for i in range(loads):
        bring(i).start()
    total[...] = jnp.zeros_like(total)
    for i in range(parts):
        bring_basis(i).wait()

    @pl.loop(0, count // GROUP)
    def _(step):
        for i in range(loads * GROUP // count):
            bring(step * (loads * GROUP // count) + i).wait()
        for u in range(GROUP):
            t = step * GROUP + u
            total[blocks[t]] += jnp.dot(values[t], arrived[places[t]], preferred_element_type=F32)

    each = BR_DEV // shares
    rows = each * total.shape[1]
    for k, out in enumerate(outs):
        share = lax.rem(me[0] + k, shares)
        steps, power = encode(total[pl.ds(share * each, each)].reshape(rows, HALF))
        out[pl.ds(0, rows)] = steps
        out[pl.ds(rows, 16)] = (
            jnp.broadcast_to(power, (16, HALF)).astype(jnp.int32).astype(jnp.int16)
        )


def tiles(me, places, blocks, values, arrived, shares, half, after):
    count, height, depth = values.shape
    rows = BR_DEV * height // shares
    inputs = [pl.BlockSpec(memory_space=pltpu.SMEM)] * 3
    inputs += [pl.BlockSpec(memory_space=pl.ANY)] * (2 + len(after))
    return pl.pallas_call(
        functools.partial(tiles_kernel, shares),
        in_specs=inputs,
        out_specs=[pl.BlockSpec(memory_space=pltpu.VMEM)] * shares,
        scratch_shapes=[
            pltpu.VMEM((BR_DEV, height, HALF), F32),
            pltpu.VMEM(values.shape, values.dtype),
            pltpu.VMEM(arrived.shape, arrived.dtype),
            pltpu.SemaphoreType.DMA((LOADS,)),
            pltpu.SemaphoreType.DMA((4,)),
        ],
        out_shape=[jax.ShapeDtypeStruct((rows + 16, HALF), jnp.int16)] * shares,
        compiler_params=pltpu.CompilerParams(vmem_limit_bytes=44 * 2**20),
        cost_estimate=pl.CostEstimate(
            flops=2 * count * height * depth * HALF,
            bytes_accessed=count * height * depth * 2 + arrived.size * 2,
            transcendentals=0,
        ),
        name=f"tiles{half}",
    )(me, places, blocks, values, arrived, *after)


def dot_t(a, b):
    return lax.dot_general(
        a, b, (((0,), (0,)), ((), ())), precision=HIGHEST, preferred_element_type=F32
    )


def dot_n(a, b):
    return jnp.dot(a, b, precision=HIGHEST, preferred_element_type=F32)


def dot_bt(a, b):
    return lax.dot_general(
        a, b, (((1,), (1,)), ((), ())), precision=HIGHEST, preferred_element_type=F32
    )


def decode(coded):
    y = None
    for ref in coded:
        rows = ref.shape[0] - 16
        power = ref[pl.ds(rows, 16)].astype(jnp.int32).astype(F32)[0:1]
        part = ref[pl.ds(0, rows)].astype(jnp.int32).astype(F32) * (jnp.exp2(power) * (1.0 / STEP))
        y = part if y is None else y + part
    return y


def gram_kernel(shares, *refs):
    coded, before, (y_out, gram_out) = refs[:shares], refs[shares:-2], refs[-2:]
    y = decode(coded)
    y_out[...] = y
    at = 0
    for ref in before:
        gram_out[pl.ds(at, HALF)] = dot_t(ref[...], y)
        at += HALF
    gram_out[pl.ds(at, HALF)] = dot_t(y, y)


def gram(coded, before):
    rows = coded[0].shape[0] - 16
    height = HALF * (len(before) + 1)
    return pl.pallas_call(
        functools.partial(gram_kernel, len(coded)),
        out_shape=(
            jax.ShapeDtypeStruct((rows, HALF), F32),
            jax.ShapeDtypeStruct((height, HALF), F32),
        ),
        compiler_params=pltpu.CompilerParams(vmem_limit_bytes=16 * 2**20),
        cost_estimate=pl.CostEstimate(
            flops=12 * rows * height * HALF, bytes_accessed=rows * HALF * 12, transcendentals=0
        ),
        name=f"gram{len(before)}",
    )(*coded, *before)


def factor64(a):
    n = a.shape[0]
    row_at = lax.broadcasted_iota(jnp.int32, (n, n), 0)
    col_at = lax.broadcasted_iota(jnp.int32, (n, n), 1)
    unit = (row_at == col_at).astype(F32)
    wide = jnp.concatenate([a, unit], axis=1)
    strips = [wide[8 * i : 8 * i + 8] for i in range(n // 8)]
    in_strip = lax.broadcasted_iota(jnp.int32, (8, 2 * n), 0)
    for j in range(n):
        b, r = divmod(j, 8)
        row = strips[b][r : r + 1]
        scaled = row / row[:, j : j + 1]
        for i in range(b, n // 8):
            if i == b and r == 7:
                continue
            column = jnp.broadcast_to(strips[i][:, j : j + 1], (8, 2 * n))
            if i == b:
                column = jnp.where(in_strip > r, column, 0.0)
            strips[i] = strips[i] - column * scaled
    wide = jnp.concatenate(strips, axis=0)
    square, inverse = wide[:, :n], wide[:, n:]
    pivots = jnp.sum(jnp.where(row_at == col_at, square, 0.0), axis=1, keepdims=True)
    scale = 1.0 / jnp.sqrt(pivots)
    return (
        jnp.where(col_at >= row_at, square, 0.0) * scale,
        jnp.where(col_at <= row_at, inverse, 0.0) * scale,
    )


def factor128(a):
    n = a.shape[0] // 2
    r00, t00 = factor64(a[:n, :n])
    r01 = dot_n(t00, a[:n, n:])
    r11, t11 = factor64(a[n:, n:] - dot_t(r01, r01))
    t10 = -dot_n(t11, dot_n(r01.T, t00))
    none = jnp.zeros((n, n), F32)
    r = jnp.concatenate(
        [jnp.concatenate([r00, r01], axis=1), jnp.concatenate([none, r11], axis=1)], axis=0
    )
    t = jnp.concatenate(
        [jnp.concatenate([t00, none], axis=1), jnp.concatenate([t10, t11], axis=1)], axis=0
    )
    return r, t


def first_kernel(scale, g_ref, y_ref, r_out, t_out, z_out):
    r, t = factor128(g_ref[...])
    r_out[...] = r
    t_out[...] = t
    z_out[...] = dot_bt(y_ref[...], t)


def first(g, y, scale):
    return pl.pallas_call(
        functools.partial(first_kernel, scale),
        out_shape=(
            jax.ShapeDtypeStruct((HALF, HALF), F32),
            jax.ShapeDtypeStruct((HALF, HALF), F32),
            jax.ShapeDtypeStruct(y.shape, F32),
        ),
        compiler_params=pltpu.CompilerParams(vmem_limit_bytes=16 * 2**20),
        cost_estimate=pl.CostEstimate(
            flops=20 * 2**20 * 1000, bytes_accessed=8 * y.size, transcendentals=0
        ),
        name="first",
    )(g, y)


def last_kernel(scale, g_ref, r_ref, t_ref, z_ref, y_ref, basis_out, triangle_out):
    r01 = dot_n(t_ref[...], g_ref[pl.ds(0, HALF)])
    r11, t11 = factor128(g_ref[pl.ds(HALF, HALF)] - dot_t(r01, r01))
    z = z_ref[...]
    basis_out[:, pl.ds(0, HALF)] = z * scale
    basis_out[:, pl.ds(HALF, HALF)] = dot_bt(y_ref[...] - dot_n(z, r01), t11) * scale
    share = 1.0 / scale
    triangle_out[pl.ds(0, HALF), pl.ds(0, HALF)] = r_ref[...] * share
    triangle_out[pl.ds(0, HALF), pl.ds(HALF, HALF)] = r01 * share
    triangle_out[pl.ds(HALF, HALF), pl.ds(0, HALF)] = jnp.zeros((HALF, HALF), F32)
    triangle_out[pl.ds(HALF, HALF), pl.ds(HALF, HALF)] = r11 * share


def last(g, r, t, z, y, scale):
    return pl.pallas_call(
        functools.partial(last_kernel, scale),
        out_shape=(
            jax.ShapeDtypeStruct((y.shape[0], 2 * HALF), F32),
            jax.ShapeDtypeStruct((2 * HALF, 2 * HALF), F32),
        ),
        compiler_params=pltpu.CompilerParams(vmem_limit_bytes=16 * 2**20),
        name="last",
    )(g, r, t, z, y)


def sum_all(part):
    axes = ("row", "col")
    n = lax.axis_size("row") * lax.axis_size("col")
    height = part.shape[0]
    pieces = lax.all_to_all(part.reshape(n, height // n, HALF), axes, 0, 0, tiled=True)
    share = jnp.sum(pieces, axis=0, keepdims=True)
    copies = jnp.broadcast_to(share, (n, height // n, HALF))
    return lax.all_to_all(copies, axes, 0, 0, tiled=True).reshape(height, HALF)


def sum_pairs(part):
    rows, cols = lax.axis_size("row"), lax.axis_size("col")
    steps = []
    for axis, size, flip in (
        ("row", rows, 1),
        ("col", cols, 1),
        ("col", cols, 3),
        ("row", rows, 2),
        ("row", rows, 6),
        ("row", rows, 8),
        ("row", rows, 24),
    ):
        part = part + lax.ppermute(part, axis, [(i, i ^ flip) for i in range(size)])
        steps.append(part)
    return steps


def local(tile_values, tile_rows, tile_source, tile_slot, send_lists, basis_blocks):
    values = tile_values[:, 0]
    blocks = tile_rows[:, 0]
    slots = send_lists.shape[3]
    places = tile_source[:, 0] * slots + tile_slot[:, 0]
    lists = send_lists.reshape(-1)
    owned = basis_blocks[:, 0]
    rows, cols = lax.axis_size("row"), lax.axis_size("col")
    cells = BR_DEV * values.shape[1] * rows
    scale = float(cells) ** 0.5
    me = lax.axis_index("col").reshape(1)

    packed = [pack(lists, owned, half) for half in range(2)]

    def product(half, after):
        arrived = lax.all_to_all(packed[half], "row", 0, 0, tiled=True)
        own, *others = tiles(me, places, blocks, values, arrived, cols, half, after)
        return [own] + [
            lax.ppermute(other, "col", [(i, (i + k) % cols) for i in range(cols)])
            for k, other in enumerate(others, 1)
        ]

    y0, g0 = gram(product(0, ()), ())
    steps = sum_pairs(g0)
    r, t, z = first(steps[-1], y0, scale)
    y1, g1 = gram(product(1, (steps[4],)), (y0,))
    return last(sum_all(g1), r, t, z, y1, scale)


def solution(mesh):
    return jax.shard_map(
        local,
        mesh=mesh,
        in_specs=(
            P("row", "col", None, None),
            P("row", "col"),
            P("row", "col"),
            P("row", "col"),
            P("row", "col", None, None),
            P("row", "col", None, None),
        ),
        out_specs=(P(("row", "col"), None), P()),
        check_vma=False,
    )
```

```python
import functools

import jax
import jax.numpy as jnp
from jax import lax
from jax.experimental import pallas as pl
from jax.experimental.pallas import tpu as pltpu
from jax.sharding import PartitionSpec as P

BR_DEV = 16
HALF = 128
GROUP = 88
LOADS = 22
STEP = 32704.0
LEAST = 2.0**-80
HIGHEST = lax.Precision.HIGHEST
F32 = jnp.float32


def pack_kernel(half, lists, owned, out, sems):
    count = out.shape[0]

    def one(i):
        return pltpu.make_async_copy(
            owned.at[lists[i], :, pl.ds(half * HALF, HALF)], out.at[i], sems.at[i]
        )

    for i in range(count):
        one(i).start()
    for i in range(count):
        one(i).wait()


def pack(lists, owned, half):
    count = lists.shape[0]
    height = owned.shape[1]
    return pl.pallas_call(
        functools.partial(pack_kernel, half),
        out_shape=jax.ShapeDtypeStruct((count, height, HALF), owned.dtype),
        in_specs=[
            pl.BlockSpec(memory_space=pltpu.SMEM),
            pl.BlockSpec(memory_space=pltpu.VMEM),
        ],
        out_specs=pl.BlockSpec(memory_space=pl.ANY),
        scratch_shapes=[pltpu.SemaphoreType.DMA((count,))],
        cost_estimate=pl.CostEstimate(
            flops=0, bytes_accessed=2 * count * height * HALF * 2, transcendentals=0
        ),
        name=f"pack{half}",
    )(lists, owned)


def encode(part):
    largest = jnp.max(jnp.abs(part), axis=0, keepdims=True)
    power = jnp.ceil(jnp.log2(jnp.maximum(largest, LEAST)))
    steps = jnp.floor(part * (jnp.exp2(-power) * STEP) + 0.5)
    return steps.astype(jnp.int32).astype(jnp.int16), power


def tiles_kernel(shares, me, places, blocks, values_hbm, arrived_hbm, *refs):
    *_, total, values, arrived, value_sems, arrived_sems = refs
    outs = refs[-5 - shares : -5]
    count, loads, parts = values.shape[0], value_sems.shape[0], arrived_sems.shape[0]

    def bring(i):
        part = pl.ds(i * (count // loads), count // loads)
        return pltpu.make_async_copy(values_hbm.at[part], values.at[part], value_sems.at[i])

    def bring_basis(i):
        part = pl.ds(i * (arrived.shape[0] // parts), arrived.shape[0] // parts)
        return pltpu.make_async_copy(arrived_hbm.at[part], arrived.at[part], arrived_sems.at[i])

    for i in range(parts):
        bring_basis(i).start()
    for i in range(loads):
        bring(i).start()
    total[...] = jnp.zeros_like(total)
    for i in range(parts):
        bring_basis(i).wait()

    @pl.loop(0, count // GROUP)
    def _(step):
        for i in range(loads * GROUP // count):
            bring(step * (loads * GROUP // count) + i).wait()
        for u in range(GROUP):
            t = step * GROUP + u
            total[blocks[t]] += jnp.dot(values[t], arrived[places[t]], preferred_element_type=F32)

    each = BR_DEV // shares
    rows = each * total.shape[1]
    for k, out in enumerate(outs):
        share = lax.rem(me[0] + k, shares)
        steps, power = encode(total[pl.ds(share * each, each)].reshape(rows, HALF))
        out[pl.ds(0, rows)] = steps
        out[pl.ds(rows, 16)] = (
            jnp.broadcast_to(power, (16, HALF)).astype(jnp.int32).astype(jnp.int16)
        )


def tiles(me, places, blocks, values, arrived, shares, half, after):
    count, height, depth = values.shape
    rows = BR_DEV * height // shares
    inputs = [pl.BlockSpec(memory_space=pltpu.SMEM)] * 3
    inputs += [pl.BlockSpec(memory_space=pl.ANY)] * (2 + len(after))
    return pl.pallas_call(
        functools.partial(tiles_kernel, shares),
        in_specs=inputs,
        out_specs=[pl.BlockSpec(memory_space=pltpu.VMEM)] * shares,
        scratch_shapes=[
            pltpu.VMEM((BR_DEV, height, HALF), F32),
            pltpu.VMEM(values.shape, values.dtype),
            pltpu.VMEM(arrived.shape, arrived.dtype),
            pltpu.SemaphoreType.DMA((LOADS,)),
            pltpu.SemaphoreType.DMA((4,)),
        ],
        out_shape=[jax.ShapeDtypeStruct((rows + 16, HALF), jnp.int16)] * shares,
        compiler_params=pltpu.CompilerParams(vmem_limit_bytes=44 * 2**20),
        cost_estimate=pl.CostEstimate(
            flops=2 * count * height * depth * HALF,
            bytes_accessed=count * height * depth * 2 + arrived.size * 2,
            transcendentals=0,
        ),
        name=f"tiles{half}",
    )(me, places, blocks, values, arrived, *after)


def dot_t(a, b):
    return lax.dot_general(
        a, b, (((0,), (0,)), ((), ())), precision=HIGHEST, preferred_element_type=F32
    )


def dot_n(a, b):
    return jnp.dot(a, b, precision=HIGHEST, preferred_element_type=F32)


def dot_bt(a, b):
    return lax.dot_general(
        a, b, (((1,), (1,)), ((), ())), precision=HIGHEST, preferred_element_type=F32
    )


def decode(coded):
    y = None
    for ref in coded:
        rows = ref.shape[0] - 16
        power = ref[pl.ds(rows, 16)].astype(jnp.int32).astype(F32)[0:1]
        part = ref[pl.ds(0, rows)].astype(jnp.int32).astype(F32) * (jnp.exp2(power) * (1.0 / STEP))
        y = part if y is None else y + part
    return y


def gram_kernel(shares, *refs):
    coded, before, (y_out, gram_out) = refs[:shares], refs[shares:-2], refs[-2:]
    y = decode(coded)
    y_out[...] = y
    at = 0
    for ref in before:
        gram_out[pl.ds(at, HALF)] = dot_t(ref[...], y)
        at += HALF
    gram_out[pl.ds(at, HALF)] = dot_t(y, y)


def gram(coded, before):
    rows = coded[0].shape[0] - 16
    height = HALF * (len(before) + 1)
    return pl.pallas_call(
        functools.partial(gram_kernel, len(coded)),
        out_shape=(
            jax.ShapeDtypeStruct((rows, HALF), F32),
            jax.ShapeDtypeStruct((height, HALF), F32),
        ),
        compiler_params=pltpu.CompilerParams(vmem_limit_bytes=16 * 2**20),
        cost_estimate=pl.CostEstimate(
            flops=12 * rows * height * HALF, bytes_accessed=rows * HALF * 12, transcendentals=0
        ),
        name=f"gram{len(before)}",
    )(*coded, *before)


def factor64(a):
    n = a.shape[0]
    row_at = lax.broadcasted_iota(jnp.int32, (n, n), 0)
    col_at = lax.broadcasted_iota(jnp.int32, (n, n), 1)
    unit = (row_at == col_at).astype(F32)
    wide = jnp.concatenate([a, unit], axis=1)
    strips = [wide[8 * i : 8 * i + 8] for i in range(n // 8)]
    in_strip = lax.broadcasted_iota(jnp.int32, (8, 2 * n), 0)
    for j in range(0, n, 4):
        b, r = divmod(j, 8)
        rows = [strips[b][r + i : r + i + 1] for i in range(4)]

        def entry(i, k, rows=rows, j=j):
            return jnp.broadcast_to(rows[i][:, j + k : j + k + 1], (1, 2 * n))

        p00, p01, p02, p03 = (entry(0, k) for k in range(4))
        p11, p12, p13 = (entry(1, k) for k in range(1, 4))
        p22, p23, p33 = entry(2, 2), entry(2, 3), entry(3, 3)
        share = 1.0 / (p00 * p11 - p01 * p01)
        w02, w12 = (p11 * p02 - p01 * p12) * share, (p00 * p12 - p01 * p02) * share
        w03, w13 = (p11 * p03 - p01 * p13) * share, (p00 * p13 - p01 * p03) * share
        q22 = p22 - (p02 * w02 + p12 * w12)
        q23 = p23 - (p02 * w03 + p12 * w13)
        q33 = p33 - (p03 * w03 + p13 * w13)
        rest = 1.0 / (q22 * q33 - q23 * q23)
        row2 = rows[2] - (w02 * rows[0] + w12 * rows[1])
        row3 = rows[3] - (w03 * rows[0] + w13 * rows[1])
        s2 = (q33 * row2 - q23 * row3) * rest
        s3 = (q22 * row3 - q23 * row2) * rest
        s0 = (p11 * rows[0] - p01 * rows[1]) * share - (w02 * s2 + w03 * s3)
        s1 = (p00 * rows[1] - p01 * rows[0]) * share - (w12 * s2 + w13 * s3)
        kept = (rows[1] - (p01 / p00) * rows[0], row2, row3 - (q23 / q22) * row2)
        for i in range(b, n // 8):
            new = strips[i]
            if i > b or r < 4:
                c0, c1, c2, c3 = (
                    jnp.broadcast_to(strips[i][:, j + k : j + k + 1], (8, 2 * n)) for k in range(4)
                )
                new = new - ((c0 * s0 + c1 * s1) + (c2 * s2 + c3 * s3))
            if i == b:
                new = jnp.where(in_strip > r + 3, new, strips[i])
                for k, row in enumerate(kept, 1):
                    new = jnp.where(in_strip == r + k, row, new)
            strips[i] = new
    wide = jnp.concatenate(strips, axis=0)
    square, inverse = wide[:, :n], wide[:, n:]
    pivots = jnp.sum(jnp.where(row_at == col_at, square, 0.0), axis=1, keepdims=True)
    scale = 1.0 / jnp.sqrt(pivots)
    return (
        jnp.where(col_at >= row_at, square, 0.0) * scale,
        jnp.where(col_at <= row_at, inverse, 0.0) * scale,
    )


def factor128(a):
    n = a.shape[0] // 2
    row_at = lax.broadcasted_iota(jnp.int32, a.shape, 0)
    col_at = lax.broadcasted_iota(jnp.int32, a.shape, 1)
    diagonal = jnp.where(row_at == col_at, a, 0.0)

    def level(squares):
        return jnp.exp2(-jnp.floor(0.5 * jnp.log2(squares)))

    along = level(jnp.sum(diagonal, axis=0, keepdims=True))
    a = a * along * level(jnp.sum(diagonal, axis=1, keepdims=True))
    r00, t00 = factor64(a[:n, :n])
    r01 = dot_n(t00, a[:n, n:])
    r11, t11 = factor64(a[n:, n:] - dot_t(r01, r01))
    t10 = -dot_n(t11, dot_n(r01.T, t00))
    none = jnp.zeros((n, n), F32)
    r = jnp.concatenate(
        [jnp.concatenate([r00, r01], axis=1), jnp.concatenate([none, r11], axis=1)], axis=0
    )
    t = jnp.concatenate(
        [jnp.concatenate([t00, none], axis=1), jnp.concatenate([t10, t11], axis=1)], axis=0
    )
    return r * (1.0 / along), t * along


def first_kernel(scale, g_ref, y_ref, r_out, t_out, z_out):
    r, t = factor128(g_ref[...])
    r_out[...] = r
    t_out[...] = t
    z_out[...] = dot_bt(y_ref[...], t)


def first(g, y, scale):
    return pl.pallas_call(
        functools.partial(first_kernel, scale),
        out_shape=(
            jax.ShapeDtypeStruct((HALF, HALF), F32),
            jax.ShapeDtypeStruct((HALF, HALF), F32),
            jax.ShapeDtypeStruct(y.shape, F32),
        ),
        compiler_params=pltpu.CompilerParams(vmem_limit_bytes=16 * 2**20),
        cost_estimate=pl.CostEstimate(
            flops=20 * 2**20 * 1000, bytes_accessed=8 * y.size, transcendentals=0
        ),
        name="first",
    )(g, y)


def last_kernel(scale, g_ref, r_ref, t_ref, z_ref, y_ref, basis_out, triangle_out):
    r01 = dot_n(t_ref[...], g_ref[pl.ds(0, HALF)])
    r11, t11 = factor128(g_ref[pl.ds(HALF, HALF)] - dot_t(r01, r01))
    z = z_ref[...]
    basis_out[:, pl.ds(0, HALF)] = z * scale
    basis_out[:, pl.ds(HALF, HALF)] = dot_bt(
        jnp.concatenate([y_ref[...], z], axis=1),
        jnp.concatenate([t11, -dot_bt(t11, r01)], axis=1) * scale,
    )
    share = 1.0 / scale
    triangle_out[pl.ds(0, HALF), pl.ds(0, HALF)] = r_ref[...] * share
    triangle_out[pl.ds(0, HALF), pl.ds(HALF, HALF)] = r01 * share
    triangle_out[pl.ds(HALF, HALF), pl.ds(0, HALF)] = jnp.zeros((HALF, HALF), F32)
    triangle_out[pl.ds(HALF, HALF), pl.ds(HALF, HALF)] = r11 * share


def last(g, r, t, z, y, scale):
    return pl.pallas_call(
        functools.partial(last_kernel, scale),
        out_shape=(
            jax.ShapeDtypeStruct((y.shape[0], 2 * HALF), F32),
            jax.ShapeDtypeStruct((2 * HALF, 2 * HALF), F32),
        ),
        compiler_params=pltpu.CompilerParams(vmem_limit_bytes=16 * 2**20),
        name="last",
    )(g, r, t, z, y)


def sum_all(part):
    axes = ("row", "col")
    n = lax.axis_size("row") * lax.axis_size("col")
    height = part.shape[0]
    pieces = lax.all_to_all(part.reshape(n, height // n, HALF), axes, 0, 0, tiled=True)
    share = jnp.sum(pieces, axis=0, keepdims=True)
    copies = jnp.broadcast_to(share, (n, height // n, HALF))
    return lax.all_to_all(copies, axes, 0, 0, tiled=True).reshape(height, HALF)


def sum_along(part):
    rows, cols = lax.axis_size("row"), lax.axis_size("col")
    steps = []
    for axis, size, stride, length in (
        ("row", rows, 1, 2),
        ("col", cols, 1, cols),
        ("row", rows, 8, 4),
        ("row", rows, 2, 4),
    ):
        arrived = [
            lax.ppermute(
                part,
                axis,
                [
                    (i, i + ((i // stride + k) % length - i // stride % length) * stride)
                    for i in range(size)
                ],
            )
            for k in range(1, length)
        ]
        if length == 2:
            part = part + arrived[0]
        else:
            part = (part + arrived[1]) + (arrived[0] + arrived[2])
        steps.append(part)
    return steps


def local(tile_values, tile_rows, tile_source, tile_slot, send_lists, basis_blocks):
    values = tile_values[:, 0]
    blocks = tile_rows[:, 0]
    slots = send_lists.shape[3]
    places = tile_source[:, 0] * slots + tile_slot[:, 0]
    lists = send_lists.reshape(-1)
    owned = basis_blocks[:, 0]
    rows, cols = lax.axis_size("row"), lax.axis_size("col")
    cells = BR_DEV * values.shape[1] * rows
    scale = float(cells) ** 0.5
    me = lax.axis_index("col").reshape(1)

    packed = [pack(lists, owned, half) for half in range(2)]

    def product(half, after):
        arrived = lax.all_to_all(packed[half], "row", 0, 0, tiled=True)
        own, *others = tiles(me, places, blocks, values, arrived, cols, half, after)
        return [own] + [
            lax.ppermute(other, "col", [(i, (i + k) % cols) for i in range(cols)])
            for k, other in enumerate(others, 1)
        ]

    y0, g0 = gram(product(0, ()), ())
    steps = sum_along(g0)
    r, t, z = first(steps[-1], y0, scale)
    y1, g1 = gram(product(1, (steps[2],)), (y0,))
    return last(sum_all(g1), r, t, z, y1, scale)


def solution(mesh):
    return jax.shard_map(
        local,
        mesh=mesh,
        in_specs=(
            P("row", "col", None, None),
            P("row", "col"),
            P("row", "col"),
            P("row", "col"),
            P("row", "col", None, None),
            P("row", "col", None, None),
        ),
        out_specs=(P(("row", "col"), None), P()),
        check_vma=False,
    )
```

```python
import functools

import jax
import jax.numpy as jnp
from jax import lax
from jax.experimental import pallas as pl
from jax.experimental.pallas import tpu as pltpu
from jax.sharding import PartitionSpec as P

BR_DEV = 16
HALF = 128
GROUP = 22
LOADS = 8
STEP = 32704.0
LEAST = 2.0**-80
HIGHEST = lax.Precision.HIGHEST
F32 = jnp.float32


def pack_kernel(half, lists, owned, out, sems):
    count, slots = out.shape[0], lists.shape[0]

    def one(i):
        return pltpu.make_async_copy(
            owned.at[lists[i % slots, i // slots], :, pl.ds(half * HALF, HALF)],
            out.at[i],
            sems.at[i],
        )

    for i in range(count):
        one(i).start()
    for i in range(count):
        one(i).wait()


def pack(lists, owned, half):
    count = lists.size
    height = owned.shape[1]
    return pl.pallas_call(
        functools.partial(pack_kernel, half),
        out_shape=jax.ShapeDtypeStruct((count, height, HALF), owned.dtype),
        in_specs=[
            pl.BlockSpec(memory_space=pltpu.SMEM),
            pl.BlockSpec(memory_space=pltpu.VMEM),
        ],
        out_specs=pl.BlockSpec(memory_space=pl.ANY),
        scratch_shapes=[pltpu.SemaphoreType.DMA((count,))],
        cost_estimate=pl.CostEstimate(
            flops=0, bytes_accessed=2 * count * height * HALF * 2, transcendentals=0
        ),
        name=f"pack{half}",
    )(lists, owned)


def encode(part):
    largest = jnp.max(jnp.abs(part), axis=0, keepdims=True)
    power = jnp.ceil(jnp.log2(jnp.maximum(largest, LEAST)))
    steps = jnp.floor(part * (jnp.exp2(-power) * STEP) + 0.5)
    return steps.astype(jnp.int32).astype(jnp.int16), power


def tiles_kernel(shares, me, places, blocks, values_hbm, arrived_hbm, *refs):
    *_, total, values, arrived, value_sems, arrived_sems = refs
    outs = refs[-5 - shares : -5]
    count, loads, parts = values.shape[0], value_sems.shape[0], arrived_sems.shape[0]
    assert count % GROUP == 0 and loads * GROUP % count == 0 and count % loads == 0

    def bring(i):
        part = pl.ds(i * (count // loads), count // loads)
        return pltpu.make_async_copy(values_hbm.at[part], values.at[part], value_sems.at[i])

    def bring_basis(i):
        part = pl.ds(i * (arrived.shape[0] // parts), arrived.shape[0] // parts)
        return pltpu.make_async_copy(arrived_hbm.at[part], arrived.at[part], arrived_sems.at[i])

    for i in range(parts):
        bring_basis(i).start()
    for i in range(loads):
        bring(i).start()
    total[...] = jnp.zeros_like(total)
    for i in range(parts):
        bring_basis(i).wait()

    @pl.loop(0, count // GROUP)
    def _(step):
        for i in range(loads * GROUP // count):
            bring(step * (loads * GROUP // count) + i).wait()
        for u in range(GROUP):
            t = step * GROUP + u
            total[blocks[t]] += jnp.dot(values[t], arrived[places[t]], preferred_element_type=F32)

    each = BR_DEV // shares
    rows = each * total.shape[1]
    for k, out in enumerate(outs):
        share = lax.rem(me[0] + k, shares)
        steps, power = encode(total[pl.ds(share * each, each)].reshape(rows, HALF))
        out[pl.ds(0, rows)] = steps
        out[pl.ds(rows, 16)] = (
            jnp.broadcast_to(power, (16, HALF)).astype(jnp.int32).astype(jnp.int16)
        )


def tiles(me, places, blocks, values, arrived, shares, half, after):
    count, height, depth = values.shape
    rows = BR_DEV * height // shares
    inputs = [pl.BlockSpec(memory_space=pltpu.SMEM)] * 3
    inputs += [pl.BlockSpec(memory_space=pl.ANY)] * (2 + len(after))
    return pl.pallas_call(
        functools.partial(tiles_kernel, shares),
        in_specs=inputs,
        out_specs=[pl.BlockSpec(memory_space=pltpu.VMEM)] * shares,
        scratch_shapes=[
            pltpu.VMEM((BR_DEV, height, HALF), F32),
            pltpu.VMEM(values.shape, values.dtype),
            pltpu.VMEM(arrived.shape, arrived.dtype),
            pltpu.SemaphoreType.DMA((LOADS,)),
            pltpu.SemaphoreType.DMA((4,)),
        ],
        out_shape=[jax.ShapeDtypeStruct((rows + 16, HALF), jnp.int16)] * shares,
        compiler_params=pltpu.CompilerParams(vmem_limit_bytes=44 * 2**20),
        cost_estimate=pl.CostEstimate(
            flops=2 * count * height * depth * HALF,
            bytes_accessed=count * height * depth * 2 + arrived.size * 2,
            transcendentals=0,
        ),
        name=f"tiles{half}",
    )(me, places, blocks, values, arrived, *after)


def dot_t(a, b):
    return lax.dot_general(
        a, b, (((0,), (0,)), ((), ())), precision=HIGHEST, preferred_element_type=F32
    )


def dot_n(a, b):
    return jnp.dot(a, b, precision=HIGHEST, preferred_element_type=F32)


def dot_bt(a, b):
    return lax.dot_general(
        a, b, (((1,), (1,)), ((), ())), precision=HIGHEST, preferred_element_type=F32
    )


def decode(coded):
    y = None
    for ref in coded:
        rows = ref.shape[0] - 16
        power = ref[pl.ds(rows, 16)].astype(jnp.int32).astype(F32)[0:1]
        part = ref[pl.ds(0, rows)].astype(jnp.int32).astype(F32) * (jnp.exp2(power) * (1.0 / STEP))
        y = part if y is None else y + part
    return y


def gram_kernel(shares, *refs):
    coded, before, (y_out, gram_out) = refs[:shares], refs[shares:-2], refs[-2:]
    y = decode(coded)
    y_out[...] = y
    at = 0
    for ref in before:
        gram_out[pl.ds(at, HALF)] = dot_t(ref[...], y)
        at += HALF
    gram_out[pl.ds(at, HALF)] = dot_t(y, y)


def gram(coded, before):
    rows = coded[0].shape[0] - 16
    height = HALF * (len(before) + 1)
    return pl.pallas_call(
        functools.partial(gram_kernel, len(coded)),
        out_shape=(
            jax.ShapeDtypeStruct((rows, HALF), F32),
            jax.ShapeDtypeStruct((height, HALF), F32),
        ),
        compiler_params=pltpu.CompilerParams(vmem_limit_bytes=16 * 2**20),
        cost_estimate=pl.CostEstimate(
            flops=12 * rows * height * HALF, bytes_accessed=rows * HALF * 12, transcendentals=0
        ),
        name=f"gram{len(before)}",
    )(*coded, *before)


def factor64(a):
    n = a.shape[0]
    row_at = lax.broadcasted_iota(jnp.int32, (n, n), 0)
    col_at = lax.broadcasted_iota(jnp.int32, (n, n), 1)
    unit = (row_at == col_at).astype(F32)
    wide = jnp.concatenate([a, unit], axis=1)
    strips = [wide[8 * i : 8 * i + 8] for i in range(n // 8)]
    in_strip = lax.broadcasted_iota(jnp.int32, (8, 2 * n), 0)
    for j in range(0, n, 4):
        b, r = divmod(j, 8)
        rows = [strips[b][r + i : r + i + 1] for i in range(4)]

        def entry(i, k, rows=rows, j=j):
            return jnp.broadcast_to(rows[i][:, j + k : j + k + 1], (1, 2 * n))

        p00, p01, p02, p03 = (entry(0, k) for k in range(4))
        p11, p12, p13 = (entry(1, k) for k in range(1, 4))
        p22, p23, p33 = entry(2, 2), entry(2, 3), entry(3, 3)
        share = 1.0 / (p00 * p11 - p01 * p01)
        w02, w12 = (p11 * p02 - p01 * p12) * share, (p00 * p12 - p01 * p02) * share
        w03, w13 = (p11 * p03 - p01 * p13) * share, (p00 * p13 - p01 * p03) * share
        q22 = p22 - (p02 * w02 + p12 * w12)
        q23 = p23 - (p02 * w03 + p12 * w13)
        q33 = p33 - (p03 * w03 + p13 * w13)
        rest = 1.0 / (q22 * q33 - q23 * q23)
        row2 = rows[2] - (w02 * rows[0] + w12 * rows[1])
        row3 = rows[3] - (w03 * rows[0] + w13 * rows[1])
        s2 = (q33 * row2 - q23 * row3) * rest
        s3 = (q22 * row3 - q23 * row2) * rest
        s0 = (p11 * rows[0] - p01 * rows[1]) * share - (w02 * s2 + w03 * s3)
        s1 = (p00 * rows[1] - p01 * rows[0]) * share - (w12 * s2 + w13 * s3)
        kept = (rows[1] - (p01 / p00) * rows[0], row2, row3 - (q23 / q22) * row2)
        for i in range(b, n // 8):
            new = strips[i]
            if i > b or r < 4:
                c0, c1, c2, c3 = (
                    jnp.broadcast_to(strips[i][:, j + k : j + k + 1], (8, 2 * n)) for k in range(4)
                )
                new = new - ((c0 * s0 + c1 * s1) + (c2 * s2 + c3 * s3))
            if i == b:
                new = jnp.where(in_strip > r + 3, new, strips[i])
                for k, row in enumerate(kept, 1):
                    new = jnp.where(in_strip == r + k, row, new)
            strips[i] = new
    wide = jnp.concatenate(strips, axis=0)
    square, inverse = wide[:, :n], wide[:, n:]
    pivots = jnp.sum(jnp.where(row_at == col_at, square, 0.0), axis=1, keepdims=True)
    scale = 1.0 / jnp.sqrt(pivots)
    return (
        jnp.where(col_at >= row_at, square, 0.0) * scale,
        jnp.where(col_at <= row_at, inverse, 0.0) * scale,
    )


def factor128(a):
    n = a.shape[0] // 2
    row_at = lax.broadcasted_iota(jnp.int32, a.shape, 0)
    col_at = lax.broadcasted_iota(jnp.int32, a.shape, 1)
    diagonal = jnp.where(row_at == col_at, a, 0.0)

    def level(squares):
        return jnp.exp2(-jnp.floor(0.5 * jnp.log2(squares)))

    along = level(jnp.sum(diagonal, axis=0, keepdims=True))
    a = a * along * level(jnp.sum(diagonal, axis=1, keepdims=True))
    r00, t00 = factor64(a[:n, :n])
    r01 = dot_n(t00, a[:n, n:])
    r11, t11 = factor64(a[n:, n:] - dot_t(r01, r01))
    t10 = -dot_n(t11, dot_n(r01.T, t00))
    none = jnp.zeros((n, n), F32)
    r = jnp.concatenate(
        [jnp.concatenate([r00, r01], axis=1), jnp.concatenate([none, r11], axis=1)], axis=0
    )
    t = jnp.concatenate(
        [jnp.concatenate([t00, none], axis=1), jnp.concatenate([t10, t11], axis=1)], axis=0
    )
    return r * (1.0 / along), t * along


def first_kernel(scale, g_ref, y_ref, r_out, t_out, z_out):
    r, t = factor128(g_ref[...])
    r_out[...] = r
    t_out[...] = t
    z_out[...] = dot_bt(y_ref[...], t)


def first(g, y, scale):
    return pl.pallas_call(
        functools.partial(first_kernel, scale),
        out_shape=(
            jax.ShapeDtypeStruct((HALF, HALF), F32),
            jax.ShapeDtypeStruct((HALF, HALF), F32),
            jax.ShapeDtypeStruct(y.shape, F32),
        ),
        compiler_params=pltpu.CompilerParams(vmem_limit_bytes=16 * 2**20),
        cost_estimate=pl.CostEstimate(
            flops=20 * 2**20 * 1000, bytes_accessed=8 * y.size, transcendentals=0
        ),
        name="first",
    )(g, y)


def last_kernel(scale, g_ref, r_ref, t_ref, z_ref, y_ref, basis_out, triangle_out):
    r01 = dot_n(t_ref[...], g_ref[pl.ds(0, HALF)])
    r11, t11 = factor128(g_ref[pl.ds(HALF, HALF)] - dot_t(r01, r01))
    z = z_ref[...]
    basis_out[:, pl.ds(0, HALF)] = z * scale
    basis_out[:, pl.ds(HALF, HALF)] = dot_bt(
        jnp.concatenate([y_ref[...], z], axis=1),
        jnp.concatenate([t11, -dot_bt(t11, r01)], axis=1) * scale,
    )
    share = 1.0 / scale
    triangle_out[pl.ds(0, HALF), pl.ds(0, HALF)] = r_ref[...] * share
    triangle_out[pl.ds(0, HALF), pl.ds(HALF, HALF)] = r01 * share
    triangle_out[pl.ds(HALF, HALF), pl.ds(0, HALF)] = jnp.zeros((HALF, HALF), F32)
    triangle_out[pl.ds(HALF, HALF), pl.ds(HALF, HALF)] = r11 * share


def last(g, r, t, z, y, scale):
    return pl.pallas_call(
        functools.partial(last_kernel, scale),
        out_shape=(
            jax.ShapeDtypeStruct((y.shape[0], 2 * HALF), F32),
            jax.ShapeDtypeStruct((2 * HALF, 2 * HALF), F32),
        ),
        compiler_params=pltpu.CompilerParams(vmem_limit_bytes=16 * 2**20),
        name="last",
    )(g, r, t, z, y)


def sum_all(part):
    axes = ("row", "col")
    n = lax.axis_size("row") * lax.axis_size("col")
    height = part.shape[0]
    pieces = lax.all_to_all(part.reshape(n, height // n, HALF), axes, 0, 0, tiled=True)
    share = jnp.sum(pieces, axis=0, keepdims=True)
    copies = jnp.broadcast_to(share, (n, height // n, HALF))
    return lax.all_to_all(copies, axes, 0, 0, tiled=True).reshape(height, HALF)


def sum_along(part):
    rows, cols = lax.axis_size("row"), lax.axis_size("col")
    steps = []
    for axis, size, stride, length in (
        ("row", rows, 1, 2),
        ("col", cols, 1, cols),
        ("row", rows, 8, 4),
        ("row", rows, 2, 4),
    ):
        arrived = [
            lax.ppermute(
                part,
                axis,
                [
                    (i, i + ((i // stride + k) % length - i // stride % length) * stride)
                    for i in range(size)
                ],
            )
            for k in range(1, length)
        ]
        if length == 2:
            part = part + arrived[0]
        else:
            part = (part + arrived[1]) + (arrived[0] + arrived[2])
        steps.append(part)
    return steps


def local(tile_values, tile_rows, tile_source, tile_slot, send_lists, basis_blocks):
    values = tile_values[:, 0]
    blocks = tile_rows[:, 0]
    slots = send_lists.shape[3]
    places = tile_source[:, 0] * slots + tile_slot[:, 0]
    lists = send_lists[0, 0].T
    owned = basis_blocks[:, 0]
    rows, cols = lax.axis_size("row"), lax.axis_size("col")
    cells = BR_DEV * values.shape[1] * rows
    scale = float(cells) ** 0.5
    me = lax.axis_index("col").reshape(1)

    packed = [pack(lists, owned, half) for half in range(2)]

    def product(half, after):
        arrived = lax.all_to_all(packed[half], "row", 0, 0, tiled=True)
        coded = tiles(me, places, blocks, values, arrived, cols, half, after)
        return [coded[0]] + [
            lax.ppermute(coded[k], "col", [(i, (i + k) % cols) for i in range(cols)])
            for k in sorted(range(1, cols), key=lambda k: -min(k, cols - k))
        ]

    y0, g0 = gram(product(0, ()), ())
    steps = sum_along(g0)
    r, t, z = first(steps[-1], y0, scale)
    y1, g1 = gram(product(1, (steps[1],)), (y0,))
    return last(sum_all(g1), r, t, z, y1, scale)


def solution(mesh):
    return jax.shard_map(
        local,
        mesh=mesh,
        in_specs=(
            P("row", "col", None, None),
            P("row", "col"),
            P("row", "col"),
            P("row", "col"),
            P("row", "col", None, None),
            P("row", "col", None, None),
        ),
        out_specs=(P(("row", "col"), None), P()),
        check_vma=False,
    )
```

```python
import functools

import jax
import jax.numpy as jnp
from jax import lax
from jax.experimental import pallas as pl
from jax.experimental.pallas import tpu as pltpu
from jax.sharding import PartitionSpec as P

BR_DEV = 16
HALF = 128
LOADS = 8
AHEAD = 2
LIMIT = 44 * 2**20
STEP = 32704.0
LEAST = 2.0**-80
HIGHEST = lax.Precision.HIGHEST
F32 = jnp.float32


def pack_kernel(half, lists, owned_hbm, out, owned, owned_sems, sems):
    count, slots = out.shape[0], lists.shape[0]

    def bring(i):
        part = owned_hbm.at[i, :, pl.ds(half * HALF, HALF)]
        return pltpu.make_async_copy(part, owned.at[i], owned_sems.at[i])

    def one(i):
        block = owned.at[lists[i % slots, i // slots]]
        return pltpu.make_async_copy(block, out.at[i], sems.at[i])

    for i in range(owned.shape[0]):
        bring(i).start()
    for i in range(owned.shape[0]):
        bring(i).wait()
    for i in range(count):
        one(i).start()
    for i in range(count):
        one(i).wait()


def pack(lists, owned, half):
    count = lists.size
    blocks, height = owned.shape[:2]
    return pl.pallas_call(
        functools.partial(pack_kernel, half),
        out_shape=jax.ShapeDtypeStruct((count, height, HALF), owned.dtype),
        in_specs=[
            pl.BlockSpec(memory_space=pltpu.SMEM),
            pl.BlockSpec(memory_space=pl.ANY),
        ],
        out_specs=pl.BlockSpec(memory_space=pl.ANY),
        scratch_shapes=[
            pltpu.VMEM((blocks, height, HALF), owned.dtype),
            pltpu.SemaphoreType.DMA((blocks,)),
            pltpu.SemaphoreType.DMA((count,)),
        ],
        cost_estimate=pl.CostEstimate(
            flops=0, bytes_accessed=2 * count * height * HALF * 2, transcendentals=0
        ),
        name=f"pack{half}",
    )(lists, owned)


def encode(part):
    largest = jnp.max(jnp.abs(part), axis=0, keepdims=True)
    power = jnp.ceil(jnp.log2(jnp.maximum(largest, LEAST)))
    steps = jnp.floor(part * (jnp.exp2(-power) * STEP) + 0.5)
    return steps.astype(jnp.int32).astype(jnp.int16), power


def tiles_kernel(shares, me, places, blocks, values_hbm, arrived_hbm, *refs):
    *_, total, values, arrived, value_sems, arrived_sems = refs
    outs = refs[-5 - shares : -5]
    count, loads, parts = values.shape[0], value_sems.shape[0], arrived_sems.shape[0]
    assert count % loads == 0 and AHEAD <= loads

    def bring(i):
        part = pl.ds(i * (count // loads), count // loads)
        return pltpu.make_async_copy(values_hbm.at[part], values.at[part], value_sems.at[i])

    def bring_basis(i):
        part = pl.ds(i * (arrived.shape[0] // parts), arrived.shape[0] // parts)
        return pltpu.make_async_copy(arrived_hbm.at[part], arrived.at[part], arrived_sems.at[i])

    for i in range(parts):
        bring_basis(i).start()
    for i in range(AHEAD):
        bring(i).start()
    total[...] = jnp.zeros_like(total)
    for i in range(parts):
        bring_basis(i).wait()

    @pl.loop(0, loads)
    def _(step):
        @pl.when(step + AHEAD < loads)
        def _():
            bring(step + AHEAD).start()

        bring(step).wait()
        for u in range(count // loads):
            t = step * (count // loads) + u
            total[blocks[t]] += jnp.dot(values[t], arrived[places[t]], preferred_element_type=F32)

    each = BR_DEV // shares
    rows = each * total.shape[1]
    for k, out in enumerate(outs):
        share = lax.rem(me[0] + k, shares)
        steps, power = encode(total[pl.ds(share * each, each)].reshape(rows, HALF))
        out[pl.ds(0, rows)] = steps
        out[pl.ds(rows, 16)] = (
            jnp.broadcast_to(power, (16, HALF)).astype(jnp.int32).astype(jnp.int16)
        )


def tiles(me, places, blocks, values, arrived, shares, half, after):
    count, height, depth = values.shape
    rows = BR_DEV * height // shares
    inputs = [pl.BlockSpec(memory_space=pltpu.SMEM)] * 3
    inputs += [pl.BlockSpec(memory_space=pl.ANY)] * (2 + len(after))
    return pl.pallas_call(
        functools.partial(tiles_kernel, shares),
        in_specs=inputs,
        out_specs=[pl.BlockSpec(memory_space=pltpu.VMEM)] * shares,
        scratch_shapes=[
            pltpu.VMEM((BR_DEV, height, HALF), F32),
            pltpu.VMEM(values.shape, values.dtype),
            pltpu.VMEM(arrived.shape, arrived.dtype),
            pltpu.SemaphoreType.DMA((LOADS,)),
            pltpu.SemaphoreType.DMA((4,)),
        ],
        out_shape=[jax.ShapeDtypeStruct((rows + 16, HALF), jnp.int16)] * shares,
        compiler_params=pltpu.CompilerParams(vmem_limit_bytes=LIMIT),
        cost_estimate=pl.CostEstimate(
            flops=2 * count * height * depth * HALF,
            bytes_accessed=count * height * depth * 2 + arrived.size * 2,
            transcendentals=0,
        ),
        name=f"tiles{half}",
    )(me, places, blocks, values, arrived, *after)


def dot_t(a, b):
    return lax.dot_general(
        a, b, (((0,), (0,)), ((), ())), precision=HIGHEST, preferred_element_type=F32
    )


def dot_n(a, b):
    return jnp.dot(a, b, precision=HIGHEST, preferred_element_type=F32)


def dot_bt(a, b):
    return lax.dot_general(
        a, b, (((1,), (1,)), ((), ())), precision=HIGHEST, preferred_element_type=F32
    )


def decode(coded):
    y = None
    for ref in coded:
        rows = ref.shape[0] - 16
        power = ref[pl.ds(rows, 16)].astype(jnp.int32).astype(F32)[0:1]
        part = ref[pl.ds(0, rows)].astype(jnp.int32).astype(F32) * (jnp.exp2(power) * (1.0 / STEP))
        y = part if y is None else y + part
    return y


def gram_kernel(shares, *refs):
    coded, before, (y_out, gram_out) = refs[:shares], refs[shares:-2], refs[-2:]
    y = decode(coded)
    y_out[...] = y
    at = 0
    for ref in before:
        gram_out[pl.ds(at, HALF)] = dot_t(ref[...], y)
        at += HALF
    gram_out[pl.ds(at, HALF)] = dot_t(y, y)


def gram(coded, before):
    rows = coded[0].shape[0] - 16
    height = HALF * (len(before) + 1)
    return pl.pallas_call(
        functools.partial(gram_kernel, len(coded)),
        out_shape=(
            jax.ShapeDtypeStruct((rows, HALF), F32),
            jax.ShapeDtypeStruct((height, HALF), F32),
        ),
        compiler_params=pltpu.CompilerParams(vmem_limit_bytes=16 * 2**20),
        cost_estimate=pl.CostEstimate(
            flops=12 * rows * height * HALF, bytes_accessed=rows * HALF * 12, transcendentals=0
        ),
        name=f"gram{len(before)}",
    )(*coded, *before)


def factor64(a):
    n = a.shape[0]
    row_at = lax.broadcasted_iota(jnp.int32, (n, n), 0)
    col_at = lax.broadcasted_iota(jnp.int32, (n, n), 1)
    unit = (row_at == col_at).astype(F32)
    wide = jnp.concatenate([a, unit], axis=1)
    strips = [wide[8 * i : 8 * i + 8] for i in range(n // 8)]
    in_strip = lax.broadcasted_iota(jnp.int32, (8, 2 * n), 0)
    for j in range(0, n, 4):
        b, r = divmod(j, 8)
        rows = [strips[b][r + i : r + i + 1] for i in range(4)]

        def entry(i, k, rows=rows, j=j):
            return jnp.broadcast_to(rows[i][:, j + k : j + k + 1], (1, 2 * n))

        p00, p01, p02, p03 = (entry(0, k) for k in range(4))
        p11, p12, p13 = (entry(1, k) for k in range(1, 4))
        p22, p23, p33 = entry(2, 2), entry(2, 3), entry(3, 3)
        share = 1.0 / (p00 * p11 - p01 * p01)
        w02, w12 = (p11 * p02 - p01 * p12) * share, (p00 * p12 - p01 * p02) * share
        w03, w13 = (p11 * p03 - p01 * p13) * share, (p00 * p13 - p01 * p03) * share
        q22 = p22 - (p02 * w02 + p12 * w12)
        q23 = p23 - (p02 * w03 + p12 * w13)
        q33 = p33 - (p03 * w03 + p13 * w13)
        rest = 1.0 / (q22 * q33 - q23 * q23)
        row2 = rows[2] - (w02 * rows[0] + w12 * rows[1])
        row3 = rows[3] - (w03 * rows[0] + w13 * rows[1])
        s2 = (q33 * row2 - q23 * row3) * rest
        s3 = (q22 * row3 - q23 * row2) * rest
        s0 = (p11 * rows[0] - p01 * rows[1]) * share - (w02 * s2 + w03 * s3)
        s1 = (p00 * rows[1] - p01 * rows[0]) * share - (w12 * s2 + w13 * s3)
        kept = (rows[1] - (p01 / p00) * rows[0], row2, row3 - (q23 / q22) * row2)
        for i in range(b, n // 8):
            new = strips[i]
            if i > b or r < 4:
                c0, c1, c2, c3 = (
                    jnp.broadcast_to(strips[i][:, j + k : j + k + 1], (8, 2 * n)) for k in range(4)
                )
                new = new - ((c0 * s0 + c1 * s1) + (c2 * s2 + c3 * s3))
            if i == b:
                new = jnp.where(in_strip > r + 3, new, strips[i])
                for k, row in enumerate(kept, 1):
                    new = jnp.where(in_strip == r + k, row, new)
            strips[i] = new
    wide = jnp.concatenate(strips, axis=0)
    square, inverse = wide[:, :n], wide[:, n:]
    pivots = jnp.sum(jnp.where(row_at == col_at, square, 0.0), axis=1, keepdims=True)
    scale = 1.0 / jnp.sqrt(pivots)
    return (
        jnp.where(col_at >= row_at, square, 0.0) * scale,
        jnp.where(col_at <= row_at, inverse, 0.0) * scale,
    )


def factor128(a):
    n = a.shape[0] // 2
    row_at = lax.broadcasted_iota(jnp.int32, a.shape, 0)
    col_at = lax.broadcasted_iota(jnp.int32, a.shape, 1)
    diagonal = jnp.where(row_at == col_at, a, 0.0)

    def level(squares):
        return jnp.exp2(-jnp.floor(0.5 * jnp.log2(squares)))

    along = level(jnp.sum(diagonal, axis=0, keepdims=True))
    a = a * along * level(jnp.sum(diagonal, axis=1, keepdims=True))
    r00, t00 = factor64(a[:n, :n])
    r01 = dot_n(t00, a[:n, n:])
    r11, t11 = factor64(a[n:, n:] - dot_t(r01, r01))
    t10 = -dot_n(t11, dot_n(r01.T, t00))
    none = jnp.zeros((n, n), F32)
    r = jnp.concatenate(
        [jnp.concatenate([r00, r01], axis=1), jnp.concatenate([none, r11], axis=1)], axis=0
    )
    t = jnp.concatenate(
        [jnp.concatenate([t00, none], axis=1), jnp.concatenate([t10, t11], axis=1)], axis=0
    )
    return r * (1.0 / along), t * along


def first_kernel(scale, g_ref, y_ref, r_out, t_out, z_out):
    r, t = factor128(g_ref[...])
    r_out[...] = r
    t_out[...] = t
    z_out[...] = dot_bt(y_ref[...], t)


def first(g, y, scale):
    return pl.pallas_call(
        functools.partial(first_kernel, scale),
        out_shape=(
            jax.ShapeDtypeStruct((HALF, HALF), F32),
            jax.ShapeDtypeStruct((HALF, HALF), F32),
            jax.ShapeDtypeStruct(y.shape, F32),
        ),
        compiler_params=pltpu.CompilerParams(vmem_limit_bytes=16 * 2**20),
        cost_estimate=pl.CostEstimate(
            flops=20 * 2**20 * 1000, bytes_accessed=8 * y.size, transcendentals=0
        ),
        name="first",
    )(g, y)


def last_kernel(scale, g_ref, r_ref, t_ref, z_ref, y_ref, basis_out, triangle_out):
    r01 = dot_n(t_ref[...], g_ref[pl.ds(0, HALF)])
    r11, t11 = factor128(g_ref[pl.ds(HALF, HALF)] - dot_t(r01, r01))
    z = z_ref[...]
    basis_out[:, pl.ds(0, HALF)] = z * scale
    basis_out[:, pl.ds(HALF, HALF)] = dot_bt(
        jnp.concatenate([y_ref[...], z], axis=1),
        jnp.concatenate([t11, -dot_bt(t11, r01)], axis=1) * scale,
    )
    share = 1.0 / scale
    triangle_out[pl.ds(0, HALF), pl.ds(0, HALF)] = r_ref[...] * share
    triangle_out[pl.ds(0, HALF), pl.ds(HALF, HALF)] = r01 * share
    triangle_out[pl.ds(HALF, HALF), pl.ds(0, HALF)] = jnp.zeros((HALF, HALF), F32)
    triangle_out[pl.ds(HALF, HALF), pl.ds(HALF, HALF)] = r11 * share


def last(g, r, t, z, y, scale):
    return pl.pallas_call(
        functools.partial(last_kernel, scale),
        out_shape=(
            jax.ShapeDtypeStruct((y.shape[0], 2 * HALF), F32),
            jax.ShapeDtypeStruct((2 * HALF, 2 * HALF), F32),
        ),
        compiler_params=pltpu.CompilerParams(vmem_limit_bytes=16 * 2**20),
        name="last",
    )(g, r, t, z, y)


def sum_all(part):
    axes = ("row", "col")
    n = lax.axis_size("row") * lax.axis_size("col")
    height = part.shape[0]
    pieces = lax.all_to_all(part.reshape(n, height // n, HALF), axes, 0, 0, tiled=True)
    share = jnp.sum(pieces, axis=0, keepdims=True)
    copies = jnp.broadcast_to(share, (n, height // n, HALF))
    return lax.all_to_all(copies, axes, 0, 0, tiled=True).reshape(height, HALF)


def sum_along(part):
    rows, cols = lax.axis_size("row"), lax.axis_size("col")
    steps = []
    for axis, size, stride, length in (
        ("row", rows, 1, 2),
        ("col", cols, 1, cols),
        ("row", rows, 8, 4),
        ("row", rows, 2, 4),
    ):
        arrived = [
            lax.ppermute(
                part,
                axis,
                [
                    (i, i + ((i // stride + k) % length - i // stride % length) * stride)
                    for i in range(size)
                ],
            )
            for k in range(1, length)
        ]
        if length == 2:
            part = part + arrived[0]
        else:
            part = (part + arrived[1]) + (arrived[0] + arrived[2])
        steps.append(part)
    return steps


def local(tile_values, tile_rows, tile_source, tile_slot, send_lists, basis_blocks):
    values = tile_values[:, 0]
    blocks = tile_rows[:, 0]
    slots = send_lists.shape[3]
    places = tile_source[:, 0] * slots + tile_slot[:, 0]
    lists = send_lists[0, 0].T
    owned = basis_blocks[:, 0]
    rows, cols = lax.axis_size("row"), lax.axis_size("col")
    cells = BR_DEV * values.shape[1] * rows
    scale = float(cells) ** 0.5
    me = lax.axis_index("col").reshape(1)

    packed = [pack(lists, owned, half) for half in range(2)]

    def product(half, after):
        arrived = lax.all_to_all(packed[half], "row", 0, 0, tiled=True)
        coded = tiles(me, places, blocks, values, arrived, cols, half, after)
        return [coded[0]] + [
            lax.ppermute(coded[k], "col", [(i, (i + k) % cols) for i in range(cols)])
            for k in sorted(range(1, cols), key=lambda k: -min(k, cols - k))
        ]

    y0, g0 = gram(product(0, ()), ())
    steps = sum_along(g0)
    r, t, z = first(steps[-1], y0, scale)
    y1, g1 = gram(product(1, (steps[1],)), (y0,))
    return last(sum_all(g1), r, t, z, y1, scale)


def solution(mesh):
    return jax.shard_map(
        local,
        mesh=mesh,
        in_specs=(
            P("row", "col", None, None),
            P("row", "col"),
            P("row", "col"),
            P("row", "col"),
            P("row", "col", None, None),
            P("row", "col", None, None),
        ),
        out_specs=(P(("row", "col"), None), P()),
        check_vma=False,
    )
```

```python
import functools

import jax
import jax.numpy as jnp
from jax import lax
from jax.experimental import pallas as pl
from jax.experimental.pallas import tpu as pltpu
from jax.sharding import PartitionSpec as P

BR_DEV = 16
HALF = 128
LOADS = 8
AHEAD = 2
LIMIT = 44 * 2**20
STEP = 32704.0
LEAST = 2.0**-80
HIGHEST = lax.Precision.HIGHEST
F32 = jnp.float32


def pack_kernel(half, lists, owned, out, sems):
    count, slots = out.shape[0], lists.shape[0]

    def one(i):
        return pltpu.make_async_copy(
            owned.at[lists[i % slots, i // slots], :, pl.ds(half * HALF, HALF)],
            out.at[i],
            sems.at[i],
        )

    for i in range(count):
        one(i).start()
    for i in range(count):
        one(i).wait()


def pack(lists, owned, half):
    count = lists.size
    height = owned.shape[1]
    return pl.pallas_call(
        functools.partial(pack_kernel, half),
        out_shape=jax.ShapeDtypeStruct((count, height, HALF), owned.dtype),
        in_specs=[
            pl.BlockSpec(memory_space=pltpu.SMEM),
            pl.BlockSpec(memory_space=pltpu.VMEM),
        ],
        out_specs=pl.BlockSpec(memory_space=pl.ANY),
        scratch_shapes=[pltpu.SemaphoreType.DMA((count,))],
        cost_estimate=pl.CostEstimate(
            flops=0, bytes_accessed=2 * count * height * HALF * 2, transcendentals=0
        ),
        name=f"pack{half}",
    )(lists, owned)


def encode(part):
    largest = jnp.max(jnp.abs(part), axis=0, keepdims=True)
    power = jnp.ceil(jnp.log2(jnp.maximum(largest, LEAST)))
    steps = jnp.floor(part * (jnp.exp2(-power) * STEP) + 0.5)
    return steps.astype(jnp.int32).astype(jnp.int16), power


def tiles_kernel(shares, me, places, blocks, values_hbm, arrived_hbm, *refs):
    *_, total, values, arrived, value_sems, arrived_sems = refs
    outs = refs[-5 - shares : -5]
    count, loads, parts = values.shape[0], value_sems.shape[0], arrived_sems.shape[0]
    assert count % loads == 0 and AHEAD <= loads

    def bring(i):
        part = pl.ds(i * (count // loads), count // loads)
        return pltpu.make_async_copy(values_hbm.at[part], values.at[part], value_sems.at[i])

    def bring_basis(i):
        part = pl.ds(i * (arrived.shape[0] // parts), arrived.shape[0] // parts)
        return pltpu.make_async_copy(arrived_hbm.at[part], arrived.at[part], arrived_sems.at[i])

    for i in range(parts):
        bring_basis(i).start()
    for i in range(AHEAD):
        bring(i).start()
    total[...] = jnp.zeros_like(total)
    for i in range(parts):
        bring_basis(i).wait()

    @pl.loop(0, loads)
    def _(step):
        @pl.when(step + AHEAD < loads)
        def _():
            bring(step + AHEAD).start()

        bring(step).wait()
        for u in range(count // loads):
            t = step * (count // loads) + u
            total[blocks[t]] += jnp.dot(values[t], arrived[places[t]], preferred_element_type=F32)

    each = BR_DEV // shares
    rows = each * total.shape[1]
    for k, out in enumerate(outs):
        share = lax.rem(me[0] + k, shares)
        steps, power = encode(total[pl.ds(share * each, each)].reshape(rows, HALF))
        out[pl.ds(0, rows)] = steps
        out[pl.ds(rows, 16)] = (
            jnp.broadcast_to(power, (16, HALF)).astype(jnp.int32).astype(jnp.int16)
        )


def tiles(me, places, blocks, values, arrived, shares, half, after):
    count, height, depth = values.shape
    rows = BR_DEV * height // shares
    inputs = [pl.BlockSpec(memory_space=pltpu.SMEM)] * 3
    inputs += [pl.BlockSpec(memory_space=pl.ANY)] * (2 + len(after))
    return pl.pallas_call(
        functools.partial(tiles_kernel, shares),
        in_specs=inputs,
        out_specs=[pl.BlockSpec(memory_space=pltpu.VMEM)] * shares,
        scratch_shapes=[
            pltpu.VMEM((BR_DEV, height, HALF), F32),
            pltpu.VMEM(values.shape, values.dtype),
            pltpu.VMEM(arrived.shape, arrived.dtype),
            pltpu.SemaphoreType.DMA((LOADS,)),
            pltpu.SemaphoreType.DMA((4,)),
        ],
        out_shape=[jax.ShapeDtypeStruct((rows + 16, HALF), jnp.int16)] * shares,
        compiler_params=pltpu.CompilerParams(vmem_limit_bytes=LIMIT),
        cost_estimate=pl.CostEstimate(
            flops=2 * count * height * depth * HALF,
            bytes_accessed=count * height * depth * 2 + arrived.size * 2,
            transcendentals=0,
        ),
        name=f"tiles{half}",
    )(me, places, blocks, values, arrived, *after)


def dot_t(a, b):
    return lax.dot_general(
        a, b, (((0,), (0,)), ((), ())), precision=HIGHEST, preferred_element_type=F32
    )


def dot_n(a, b):
    return jnp.dot(a, b, precision=HIGHEST, preferred_element_type=F32)


def dot_bt(a, b):
    return lax.dot_general(
        a, b, (((1,), (1,)), ((), ())), precision=HIGHEST, preferred_element_type=F32
    )


def decode(coded):
    y = None
    for ref in coded:
        rows = ref.shape[0] - 16
        power = ref[pl.ds(rows, 16)].astype(jnp.int32).astype(F32)[0:1]
        part = ref[pl.ds(0, rows)].astype(jnp.int32).astype(F32) * (jnp.exp2(power) * (1.0 / STEP))
        y = part if y is None else y + part
    return y


def gram_first_kernel(shares, *refs):
    coded, (y_out, gram_out) = refs[:shares], refs[shares:]
    y = decode(coded)
    y_out[...] = y
    gram_out[...] = dot_t(y, y)


def gram_last_kernel(shares, core, before, *refs):
    coded, (y_out, mine_out, other_out) = refs[:shares], refs[-3:]
    y = decode(coded)
    y_out[...] = y
    cross, square = dot_t(before[...], y), dot_t(y, y)
    mine_out[...] = jnp.where(core[0] == 0, cross, square)
    other_out[...] = jnp.where(core[0] == 0, square, cross)


def gram_call(kernel, operands, in_specs, rows, grams, name):
    return pl.pallas_call(
        kernel,
        in_specs=in_specs,
        out_shape=[jax.ShapeDtypeStruct((rows, HALF), F32)]
        + [jax.ShapeDtypeStruct((HALF, HALF), F32)] * grams,
        compiler_params=pltpu.CompilerParams(vmem_limit_bytes=16 * 2**20),
        cost_estimate=pl.CostEstimate(
            flops=12 * rows * grams * HALF * HALF, bytes_accessed=rows * HALF * 12, transcendentals=0
        ),
        name=name,
    )(*operands)


def gram_first(coded):
    rows = coded[0].shape[0] - 16
    whole = pl.BlockSpec(memory_space=pltpu.VMEM)
    kernel = functools.partial(gram_first_kernel, len(coded))
    return gram_call(kernel, coded, [whole] * len(coded), rows, 1, "gram0")


def gram_last(coded, before, core, after):
    rows = coded[0].shape[0] - 16
    whole = pl.BlockSpec(memory_space=pltpu.VMEM)
    kernel = functools.partial(gram_last_kernel, len(coded))
    specs = [pl.BlockSpec(memory_space=pltpu.SMEM), whole]
    specs += [whole] * len(coded) + [pl.BlockSpec(memory_space=pl.ANY)]
    return gram_call(kernel, [core, before, *coded, after], specs, rows, 2, "gram1")


def factor64(a):
    n = a.shape[0]
    row_at = lax.broadcasted_iota(jnp.int32, (n, n), 0)
    col_at = lax.broadcasted_iota(jnp.int32, (n, n), 1)
    unit = (row_at == col_at).astype(F32)
    wide = jnp.concatenate([a, unit], axis=1)
    strips = [wide[8 * i : 8 * i + 8] for i in range(n // 8)]
    in_strip = lax.broadcasted_iota(jnp.int32, (8, 2 * n), 0)
    for j in range(0, n, 4):
        b, r = divmod(j, 8)
        rows = [strips[b][r + i : r + i + 1] for i in range(4)]

        def entry(i, k, rows=rows, j=j):
            return jnp.broadcast_to(rows[i][:, j + k : j + k + 1], (1, 2 * n))

        p00, p01, p02, p03 = (entry(0, k) for k in range(4))
        p11, p12, p13 = (entry(1, k) for k in range(1, 4))
        p22, p23, p33 = entry(2, 2), entry(2, 3), entry(3, 3)
        share = 1.0 / (p00 * p11 - p01 * p01)
        w02, w12 = (p11 * p02 - p01 * p12) * share, (p00 * p12 - p01 * p02) * share
        w03, w13 = (p11 * p03 - p01 * p13) * share, (p00 * p13 - p01 * p03) * share
        q22 = p22 - (p02 * w02 + p12 * w12)
        q23 = p23 - (p02 * w03 + p12 * w13)
        q33 = p33 - (p03 * w03 + p13 * w13)
        rest = 1.0 / (q22 * q33 - q23 * q23)
        row2 = rows[2] - (w02 * rows[0] + w12 * rows[1])
        row3 = rows[3] - (w03 * rows[0] + w13 * rows[1])
        s2 = (q33 * row2 - q23 * row3) * rest
        s3 = (q22 * row3 - q23 * row2) * rest
        s0 = (p11 * rows[0] - p01 * rows[1]) * share - (w02 * s2 + w03 * s3)
        s1 = (p00 * rows[1] - p01 * rows[0]) * share - (w12 * s2 + w13 * s3)
        kept = (rows[1] - (p01 / p00) * rows[0], row2, row3 - (q23 / q22) * row2)
        for i in range(b, n // 8):
            new = strips[i]
            if i > b or r < 4:
                c0, c1, c2, c3 = (
                    jnp.broadcast_to(strips[i][:, j + k : j + k + 1], (8, 2 * n)) for k in range(4)
                )
                new = new - ((c0 * s0 + c1 * s1) + (c2 * s2 + c3 * s3))
            if i == b:
                new = jnp.where(in_strip > r + 3, new, strips[i])
                for k, row in enumerate(kept, 1):
                    new = jnp.where(in_strip == r + k, row, new)
            strips[i] = new
    wide = jnp.concatenate(strips, axis=0)
    square, inverse = wide[:, :n], wide[:, n:]
    pivots = jnp.sum(jnp.where(row_at == col_at, square, 0.0), axis=1, keepdims=True)
    scale = 1.0 / jnp.sqrt(pivots)
    return (
        jnp.where(col_at >= row_at, square, 0.0) * scale,
        jnp.where(col_at <= row_at, inverse, 0.0) * scale,
    )


def factor128(a):
    n = a.shape[0] // 2
    row_at = lax.broadcasted_iota(jnp.int32, a.shape, 0)
    col_at = lax.broadcasted_iota(jnp.int32, a.shape, 1)
    diagonal = jnp.where(row_at == col_at, a, 0.0)

    def level(squares):
        return jnp.exp2(-jnp.floor(0.5 * jnp.log2(squares)))

    along = level(jnp.sum(diagonal, axis=0, keepdims=True))
    a = a * along * level(jnp.sum(diagonal, axis=1, keepdims=True))
    r00, t00 = factor64(a[:n, :n])
    r01 = dot_n(t00, a[:n, n:])
    r11, t11 = factor64(a[n:, n:] - dot_t(r01, r01))
    t10 = -dot_n(t11, dot_n(r01.T, t00))
    none = jnp.zeros((n, n), F32)
    r = jnp.concatenate(
        [jnp.concatenate([r00, r01], axis=1), jnp.concatenate([none, r11], axis=1)], axis=0
    )
    t = jnp.concatenate(
        [jnp.concatenate([t00, none], axis=1), jnp.concatenate([t10, t11], axis=1)], axis=0
    )
    return r * (1.0 / along), t * along


def first_kernel(scale, g_ref, y_ref, r_out, t_out, z_out):
    r, t = factor128(g_ref[...])
    r_out[...] = r
    t_out[...] = t
    z_out[...] = dot_bt(y_ref[...], t)


def first(g, y, scale):
    return pl.pallas_call(
        functools.partial(first_kernel, scale),
        out_shape=(
            jax.ShapeDtypeStruct((HALF, HALF), F32),
            jax.ShapeDtypeStruct((HALF, HALF), F32),
            jax.ShapeDtypeStruct(y.shape, F32),
        ),
        compiler_params=pltpu.CompilerParams(vmem_limit_bytes=16 * 2**20),
        cost_estimate=pl.CostEstimate(
            flops=20 * 2**20 * 1000, bytes_accessed=8 * y.size, transcendentals=0
        ),
        name="first",
    )(g, y)


def last_kernel(scale, core, mine, other, r_ref, t_ref, z_ref, y_ref, basis_out, triangle_out):
    cross = jnp.where(core[0] == 0, mine[...], other[...])
    square = jnp.where(core[0] == 0, other[...], mine[...])
    r01 = dot_n(t_ref[...], cross)
    r11, t11 = factor128(square - dot_t(r01, r01))
    z = z_ref[...]
    basis_out[:, pl.ds(0, HALF)] = z * scale
    basis_out[:, pl.ds(HALF, HALF)] = dot_bt(
        jnp.concatenate([y_ref[...], z], axis=1),
        jnp.concatenate([t11, -dot_bt(t11, r01)], axis=1) * scale,
    )
    share = 1.0 / scale
    triangle_out[pl.ds(0, HALF), pl.ds(0, HALF)] = r_ref[...] * share
    triangle_out[pl.ds(0, HALF), pl.ds(HALF, HALF)] = r01 * share
    triangle_out[pl.ds(HALF, HALF), pl.ds(0, HALF)] = jnp.zeros((HALF, HALF), F32)
    triangle_out[pl.ds(HALF, HALF), pl.ds(HALF, HALF)] = r11 * share


def last(core, mine, other, r, t, z, y, scale):
    return pl.pallas_call(
        functools.partial(last_kernel, scale),
        in_specs=[pl.BlockSpec(memory_space=pltpu.SMEM)]
        + [pl.BlockSpec(memory_space=pltpu.VMEM)] * 6,
        out_shape=(
            jax.ShapeDtypeStruct((y.shape[0], 2 * HALF), F32),
            jax.ShapeDtypeStruct((2 * HALF, 2 * HALF), F32),
        ),
        compiler_params=pltpu.CompilerParams(vmem_limit_bytes=16 * 2**20),
        name="last",
    )(core, mine, other, r, t, z, y)


def swap_cores(part):
    return lax.ppermute(part, "row", [(i, i ^ 1) for i in range(lax.axis_size("row"))])


def sum_chips(part):
    rows, cols = lax.axis_size("row"), lax.axis_size("col")
    steps = []
    for axis, size, stride in (("col", cols, 1), ("row", rows, 8), ("row", rows, 2)):
        two, one, three = (
            lax.ppermute(
                part,
                axis,
                [(i, i + ((i // stride + k) % 4 - i // stride % 4) * stride) for i in range(size)],
            )
            for k in (2, 1, 3)
        )
        part = (part + two) + (one + three)
        steps.append(part)
    return steps


def local(tile_values, tile_rows, tile_source, tile_slot, send_lists, basis_blocks):
    values = tile_values[:, 0]
    blocks = tile_rows[:, 0]
    slots = send_lists.shape[3]
    places = tile_source[:, 0] * slots + tile_slot[:, 0]
    lists = send_lists[0, 0].T
    owned = basis_blocks[:, 0]
    rows, cols = lax.axis_size("row"), lax.axis_size("col")
    cells = BR_DEV * values.shape[1] * rows
    scale = float(cells) ** 0.5
    me = lax.axis_index("col").reshape(1)

    packed = [pack(lists, owned, half) for half in range(2)]

    def product(half, after):
        arrived = lax.all_to_all(packed[half], "row", 0, 0, tiled=True)
        coded = tiles(me, places, blocks, values, arrived, cols, half, after)
        return [coded[0]] + [
            lax.ppermute(coded[k], "col", [(i, (i + k) % cols) for i in range(cols)])
            for k in sorted(range(1, cols), key=lambda k: -min(k, cols - k))
        ]

    core = lax.rem(lax.axis_index("row"), 2).reshape(1)
    y0, g0 = gram_first(product(0, ()))
    steps = sum_chips(g0 + swap_cores(g0))
    r, t, z = first(steps[-1], y0, scale)
    y1, mine, other = gram_last(product(1, (steps[1],)), y0, core, z)
    mine = sum_chips(mine + swap_cores(other))[-1]
    return last(core, mine, swap_cores(mine), r, t, z, y1, scale)


def solution(mesh):
    return jax.shard_map(
        local,
        mesh=mesh,
        in_specs=(
            P("row", "col", None, None),
            P("row", "col"),
            P("row", "col"),
            P("row", "col"),
            P("row", "col", None, None),
            P("row", "col", None, None),
        ),
        out_specs=(P(("row", "col"), None), P()),
        check_vma=False,
    )
```

```python
import functools

import jax
import jax.numpy as jnp
from jax import lax
from jax.experimental import pallas as pl
from jax.experimental.pallas import tpu as pltpu
from jax.sharding import PartitionSpec as P

BR_DEV = 16
HALF = 128
LOADS = 8
AHEAD = 2
LIMIT = 44 * 2**20
STEP = 32704.0
LEAST = 2.0**-80
HIGHEST = lax.Precision.HIGHEST
F32 = jnp.float32


def pack_kernel(half, lists, owned, out, sems):
    count, slots = out.shape[0], lists.shape[0]

    def one(i):
        return pltpu.make_async_copy(
            owned.at[lists[i % slots, i // slots], :, pl.ds(half * HALF, HALF)],
            out.at[i],
            sems.at[i],
        )

    for i in range(count):
        one(i).start()
    for i in range(count):
        one(i).wait()


def pack(lists, owned, half):
    count = lists.size
    height = owned.shape[1]
    return pl.pallas_call(
        functools.partial(pack_kernel, half),
        out_shape=jax.ShapeDtypeStruct((count, height, HALF), owned.dtype),
        in_specs=[
            pl.BlockSpec(memory_space=pltpu.SMEM),
            pl.BlockSpec(memory_space=pltpu.VMEM),
        ],
        out_specs=pl.BlockSpec(memory_space=pl.ANY),
        scratch_shapes=[pltpu.SemaphoreType.DMA((count,))],
        cost_estimate=pl.CostEstimate(
            flops=0, bytes_accessed=2 * count * height * HALF * 2, transcendentals=0
        ),
        name=f"pack{half}",
    )(lists, owned)


def encode(part):
    largest = jnp.max(jnp.abs(part), axis=0, keepdims=True)
    power = jnp.ceil(jnp.log2(jnp.maximum(largest, LEAST)))
    steps = jnp.floor(part * (jnp.exp2(-power) * STEP) + 0.5)
    return steps.astype(jnp.int32).astype(jnp.int16), power


def tiles_kernel(shares, me, places, blocks, values_hbm, arrived_hbm, *refs):
    *_, total, values, arrived, value_sems, arrived_sems = refs
    outs = refs[-5 - shares : -5]
    count, loads, parts = values.shape[0], value_sems.shape[0], arrived_sems.shape[0]
    assert count % loads == 0 and AHEAD <= loads

    def bring(i):
        part = pl.ds(i * (count // loads), count // loads)
        return pltpu.make_async_copy(values_hbm.at[part], values.at[part], value_sems.at[i])

    def bring_basis(i):
        part = pl.ds(i * (arrived.shape[0] // parts), arrived.shape[0] // parts)
        return pltpu.make_async_copy(arrived_hbm.at[part], arrived.at[part], arrived_sems.at[i])

    for i in range(parts):
        bring_basis(i).start()
    for i in range(AHEAD):
        bring(i).start()
    total[...] = jnp.zeros_like(total)
    for i in range(parts):
        bring_basis(i).wait()

    @pl.loop(0, loads)
    def _(step):
        @pl.when(step + AHEAD < loads)
        def _():
            bring(step + AHEAD).start()

        bring(step).wait()
        for u in range(count // loads):
            t = step * (count // loads) + u
            total[blocks[t]] += jnp.dot(values[t], arrived[places[t]], preferred_element_type=F32)

    each = BR_DEV // shares
    rows = each * total.shape[1]
    for k, out in enumerate(outs):
        share = lax.rem(me[0] + k, shares)
        steps, power = encode(total[pl.ds(share * each, each)].reshape(rows, HALF))
        out[pl.ds(0, rows)] = steps
        out[pl.ds(rows, 16)] = (
            jnp.broadcast_to(power, (16, HALF)).astype(jnp.int32).astype(jnp.int16)
        )


def tiles(me, places, blocks, values, arrived, shares, half, after):
    count, height, depth = values.shape
    rows = BR_DEV * height // shares
    inputs = [pl.BlockSpec(memory_space=pltpu.SMEM)] * 3
    inputs += [pl.BlockSpec(memory_space=pl.ANY)] * (2 + len(after))
    return pl.pallas_call(
        functools.partial(tiles_kernel, shares),
        in_specs=inputs,
        out_specs=[pl.BlockSpec(memory_space=pltpu.VMEM)] * shares,
        scratch_shapes=[
            pltpu.VMEM((BR_DEV, height, HALF), F32),
            pltpu.VMEM(values.shape, values.dtype),
            pltpu.VMEM(arrived.shape, arrived.dtype),
            pltpu.SemaphoreType.DMA((LOADS,)),
            pltpu.SemaphoreType.DMA((4,)),
        ],
        out_shape=[jax.ShapeDtypeStruct((rows + 16, HALF), jnp.int16)] * shares,
        compiler_params=pltpu.CompilerParams(vmem_limit_bytes=LIMIT),
        cost_estimate=pl.CostEstimate(
            flops=2 * count * height * depth * HALF,
            bytes_accessed=count * height * depth * 2 + arrived.size * 2,
            transcendentals=0,
        ),
        name=f"tiles{half}",
    )(me, places, blocks, values, arrived, *after)


def dot_t(a, b):
    return lax.dot_general(
        a, b, (((0,), (0,)), ((), ())), precision=HIGHEST, preferred_element_type=F32
    )


def dot_n(a, b):
    return jnp.dot(a, b, precision=HIGHEST, preferred_element_type=F32)


def dot_bt(a, b):
    return lax.dot_general(
        a, b, (((1,), (1,)), ((), ())), precision=HIGHEST, preferred_element_type=F32
    )


def decode(coded):
    y = None
    for ref in coded:
        rows = ref.shape[0] - 16
        power = ref[pl.ds(rows, 16)].astype(jnp.int32).astype(F32)[0:1]
        part = ref[pl.ds(0, rows)].astype(jnp.int32).astype(F32) * (jnp.exp2(power) * (1.0 / STEP))
        y = part if y is None else y + part
    return y


def gram_kernel(shares, *refs):
    coded, before, (y_out, gram_out) = refs[:shares], refs[shares:-2], refs[-2:]
    y = decode(coded)
    y_out[...] = y
    at = 0
    for ref in before:
        gram_out[pl.ds(at, HALF)] = dot_t(ref[...], y)
        at += HALF
    gram_out[pl.ds(at, HALF)] = dot_t(y, y)


def gram(coded, before):
    rows = coded[0].shape[0] - 16
    height = HALF * (len(before) + 1)
    return pl.pallas_call(
        functools.partial(gram_kernel, len(coded)),
        out_shape=(
            jax.ShapeDtypeStruct((rows, HALF), F32),
            jax.ShapeDtypeStruct((height, HALF), F32),
        ),
        compiler_params=pltpu.CompilerParams(vmem_limit_bytes=16 * 2**20),
        cost_estimate=pl.CostEstimate(
            flops=12 * rows * height * HALF, bytes_accessed=rows * HALF * 12, transcendentals=0
        ),
        name=f"gram{len(before)}",
    )(*coded, *before)


def factor64(a):
    n = a.shape[0]
    row_at = lax.broadcasted_iota(jnp.int32, (n, n), 0)
    col_at = lax.broadcasted_iota(jnp.int32, (n, n), 1)
    unit = (row_at == col_at).astype(F32)
    wide = jnp.concatenate([a, unit], axis=1)
    strips = [wide[8 * i : 8 * i + 8] for i in range(n // 8)]
    in_strip = lax.broadcasted_iota(jnp.int32, (8, 2 * n), 0)
    for j in range(0, n, 4):
        b, r = divmod(j, 8)
        rows = [strips[b][r + i : r + i + 1] for i in range(4)]

        def entry(i, k, rows=rows, j=j):
            return jnp.broadcast_to(rows[i][:, j + k : j + k + 1], (1, 2 * n))

        p00, p01, p02, p03 = (entry(0, k) for k in range(4))
        p11, p12, p13 = (entry(1, k) for k in range(1, 4))
        p22, p23, p33 = entry(2, 2), entry(2, 3), entry(3, 3)
        share = 1.0 / (p00 * p11 - p01 * p01)
        w02, w12 = (p11 * p02 - p01 * p12) * share, (p00 * p12 - p01 * p02) * share
        w03, w13 = (p11 * p03 - p01 * p13) * share, (p00 * p13 - p01 * p03) * share
        q22 = p22 - (p02 * w02 + p12 * w12)
        q23 = p23 - (p02 * w03 + p12 * w13)
        q33 = p33 - (p03 * w03 + p13 * w13)
        rest = 1.0 / (q22 * q33 - q23 * q23)
        row2 = rows[2] - (w02 * rows[0] + w12 * rows[1])
        row3 = rows[3] - (w03 * rows[0] + w13 * rows[1])
        s2 = (q33 * row2 - q23 * row3) * rest
        s3 = (q22 * row3 - q23 * row2) * rest
        s0 = (p11 * rows[0] - p01 * rows[1]) * share - (w02 * s2 + w03 * s3)
        s1 = (p00 * rows[1] - p01 * rows[0]) * share - (w12 * s2 + w13 * s3)
        kept = (rows[1] - (p01 / p00) * rows[0], row2, row3 - (q23 / q22) * row2)
        for i in range(b, n // 8):
            new = strips[i]
            if i > b or r < 4:
                c0, c1, c2, c3 = (
                    jnp.broadcast_to(strips[i][:, j + k : j + k + 1], (8, 2 * n)) for k in range(4)
                )
                new = new - ((c0 * s0 + c1 * s1) + (c2 * s2 + c3 * s3))
            if i == b:
                new = jnp.where(in_strip > r + 3, new, strips[i])
                for k, row in enumerate(kept, 1):
                    new = jnp.where(in_strip == r + k, row, new)
            strips[i] = new
    wide = jnp.concatenate(strips, axis=0)
    square, inverse = wide[:, :n], wide[:, n:]
    pivots = jnp.sum(jnp.where(row_at == col_at, square, 0.0), axis=1, keepdims=True)
    scale = 1.0 / jnp.sqrt(pivots)
    return (
        jnp.where(col_at >= row_at, square, 0.0) * scale,
        jnp.where(col_at <= row_at, inverse, 0.0) * scale,
    )


def factor128(a):
    n = a.shape[0] // 2
    row_at = lax.broadcasted_iota(jnp.int32, a.shape, 0)
    col_at = lax.broadcasted_iota(jnp.int32, a.shape, 1)
    diagonal = jnp.where(row_at == col_at, a, 0.0)

    def level(squares):
        return jnp.exp2(-jnp.floor(0.5 * jnp.log2(squares)))

    along = level(jnp.sum(diagonal, axis=0, keepdims=True))
    a = a * along * level(jnp.sum(diagonal, axis=1, keepdims=True))
    r00, t00 = factor64(a[:n, :n])
    r01 = dot_n(t00, a[:n, n:])
    r11, t11 = factor64(a[n:, n:] - dot_t(r01, r01))
    t10 = -dot_n(t11, dot_n(r01.T, t00))
    none = jnp.zeros((n, n), F32)
    r = jnp.concatenate(
        [jnp.concatenate([r00, r01], axis=1), jnp.concatenate([none, r11], axis=1)], axis=0
    )
    t = jnp.concatenate(
        [jnp.concatenate([t00, none], axis=1), jnp.concatenate([t10, t11], axis=1)], axis=0
    )
    return r * (1.0 / along), t * along


def first_kernel(scale, g_ref, y_ref, r_out, t_out, z_out):
    r, t = factor128(g_ref[...])
    r_out[...] = r
    t_out[...] = t
    z_out[...] = dot_bt(y_ref[...], t)


def first(g, y, scale):
    return pl.pallas_call(
        functools.partial(first_kernel, scale),
        out_shape=(
            jax.ShapeDtypeStruct((HALF, HALF), F32),
            jax.ShapeDtypeStruct((HALF, HALF), F32),
            jax.ShapeDtypeStruct(y.shape, F32),
        ),
        compiler_params=pltpu.CompilerParams(vmem_limit_bytes=16 * 2**20),
        cost_estimate=pl.CostEstimate(
            flops=20 * 2**20 * 1000, bytes_accessed=8 * y.size, transcendentals=0
        ),
        name="first",
    )(g, y)


def last_kernel(scale, g_ref, r_ref, t_ref, z_ref, y_ref, basis_out, triangle_out):
    r01 = dot_n(t_ref[...], g_ref[pl.ds(0, HALF)])
    r11, t11 = factor128(g_ref[pl.ds(HALF, HALF)] - dot_t(r01, r01))
    z = z_ref[...]
    basis_out[:, pl.ds(0, HALF)] = z * scale
    basis_out[:, pl.ds(HALF, HALF)] = dot_bt(
        jnp.concatenate([y_ref[...], z], axis=1),
        jnp.concatenate([t11, -dot_bt(t11, r01)], axis=1) * scale,
    )
    share = 1.0 / scale
    triangle_out[pl.ds(0, HALF), pl.ds(0, HALF)] = r_ref[...] * share
    triangle_out[pl.ds(0, HALF), pl.ds(HALF, HALF)] = r01 * share
    triangle_out[pl.ds(HALF, HALF), pl.ds(0, HALF)] = jnp.zeros((HALF, HALF), F32)
    triangle_out[pl.ds(HALF, HALF), pl.ds(HALF, HALF)] = r11 * share


def last(g, r, t, z, y, scale):
    return pl.pallas_call(
        functools.partial(last_kernel, scale),
        out_shape=(
            jax.ShapeDtypeStruct((y.shape[0], 2 * HALF), F32),
            jax.ShapeDtypeStruct((2 * HALF, 2 * HALF), F32),
        ),
        compiler_params=pltpu.CompilerParams(vmem_limit_bytes=16 * 2**20),
        name="last",
    )(g, r, t, z, y)


def sum_all(part):
    axes = ("row", "col")
    n = lax.axis_size("row") * lax.axis_size("col")
    height = part.shape[0]
    pieces = lax.all_to_all(part.reshape(n, height // n, HALF), axes, 0, 0, tiled=True)
    share = jnp.sum(pieces, axis=0, keepdims=True)
    copies = jnp.broadcast_to(share, (n, height // n, HALF))
    return lax.all_to_all(copies, axes, 0, 0, tiled=True).reshape(height, HALF)


def sum_along(part):
    rows, cols = lax.axis_size("row"), lax.axis_size("col")
    steps = []
    for axis, size, stride, length in (
        ("row", rows, 1, 2),
        ("col", cols, 1, cols),
        ("row", rows, 8, 4),
        ("row", rows, 2, 4),
    ):
        arrived = [
            lax.ppermute(
                part,
                axis,
                [
                    (i, i + ((i // stride + k) % length - i // stride % length) * stride)
                    for i in range(size)
                ],
            )
            for k in range(1, length)
        ]
        if length == 2:
            part = part + arrived[0]
        else:
            part = (part + arrived[1]) + (arrived[0] + arrived[2])
        steps.append(part)
    return steps


def local(tile_values, tile_rows, tile_source, tile_slot, send_lists, basis_blocks):
    values = tile_values[:, 0]
    blocks = tile_rows[:, 0]
    slots = send_lists.shape[3]
    places = tile_source[:, 0] * slots + tile_slot[:, 0]
    lists = send_lists[0, 0].T
    owned = basis_blocks[:, 0]
    rows, cols = lax.axis_size("row"), lax.axis_size("col")
    cells = BR_DEV * values.shape[1] * rows
    scale = float(cells) ** 0.5
    me = lax.axis_index("col").reshape(1)

    packed = [pack(lists, owned, half) for half in range(2)]

    def product(half, after):
        arrived = lax.all_to_all(packed[half], "row", 0, 0, tiled=True)
        coded = tiles(me, places, blocks, values, arrived, cols, half, after)
        return [coded[0]] + [
            lax.ppermute(coded[k], "col", [(i, (i + k) % cols) for i in range(cols)])
            for k in sorted(range(1, cols), key=lambda k: -min(k, cols - k))
        ]

    y0, g0 = gram(product(0, ()), ())
    steps = sum_along(g0)
    r, t, z = first(steps[-1], y0, scale)
    y1, g1 = gram(product(1, (steps[1],)), (y0,))
    return last(sum_all(g1), r, t, z, y1, scale)


def solution(mesh):
    return jax.shard_map(
        local,
        mesh=mesh,
        in_specs=(
            P("row", "col", None, None),
            P("row", "col"),
            P("row", "col"),
            P("row", "col"),
            P("row", "col", None, None),
            P("row", "col", None, None),
        ),
        out_specs=(P(("row", "col"), None), P()),
        check_vma=False,
    )
```
